32 devices in a mesh: fsdp: 16 (over z, x, core), seq: 2 (over y).
Axes of the slice: x: 2, y: 2, z: 4, core: 2. Of those that a mesh axis runs over, the one named last changes fastest.
Arguments:
- tokens: bfloat16 [4096, 1024], P(('fsdp', 'seq')), may hold values from -6 to 6
- norm_gain: bfloat16 [1024], P(('fsdp', 'seq')), may hold values from 0.5 to 2
- w_query: bfloat16 [1024, 2048], P(('fsdp', 'seq')), may hold values from -0.1875 to 0.1875
- key_projection_weight: bfloat16 [1024, 1024], P(('fsdp', 'seq')), may hold values from -0.1875 to 0.1875
- value_projection_weight: bfloat16 [1024, 1024], P(('fsdp', 'seq')), may hold values from -0.1875 to 0.1875
- w_output: bfloat16 [2048, 1024], P(('fsdp', 'seq')), may hold values from -1 to 1
- query_gain: bfloat16 [128], P(('fsdp', 'seq')), may hold values from 0.5 to 1.5
- key_gain: bfloat16 [128], P(('fsdp', 'seq')), may hold values from 0.5 to 1.5
- mlp_gain: bfloat16 [1024], P(('fsdp', 'seq')), may hold values from 0.5 to 2
- w_gate: bfloat16 [1024, 3072], P(('fsdp', 'seq')), may hold values from -0.1875 to 0.1875
- w_up: bfloat16 [1024, 3072], P(('fsdp', 'seq')), may hold values from -0.1875 to 0.1875
- w_down: bfloat16 [3072, 1024], P(('fsdp', 'seq')), may hold values from -0.21875 to 0.21875
- lengths: int32 [16, 4], P('fsdp'), may hold values from 1 to 192, 256 in all within a row
- seq_order: int32 [16, 4], P('fsdp'), may hold values from 0 to 3, each once within a row
- cotangent: bfloat16 [4096, 1024], P(('fsdp', 'seq')), may hold values from -6 to 6
Outputs:
- result: bfloat16 [4096, 1024], P(('fsdp', 'seq'))
- grad_tokens: float32 [4096, 1024], P(('fsdp', 'seq'))
- grad_norm_gain: float32 [1024], P(('fsdp', 'seq'))
- grad_w_query: float32 [1024, 2048], P(('fsdp', 'seq'))
- grad_w_key: float32 [1024, 1024], P(('fsdp', 'seq'))
- grad_w_value: float32 [1024, 1024], P(('fsdp', 'seq'))
- grad_w_output: float32 [2048, 1024], P(('fsdp', 'seq'))
- grad_query_gain: float32 [128], P(('fsdp', 'seq'))
- key_gain_gradient: float32 [128], P(('fsdp', 'seq'))
- grad_mlp_gain: float32 [1024], P(('fsdp', 'seq'))
- grad_w_gate: float32 [1024, 3072], P(('fsdp', 'seq'))
- grad_w_up: float32 [1024, 3072], P(('fsdp', 'seq'))
- grad_w_down: float32 [3072, 1024], P(('fsdp', 'seq'))
The draws below stay inside these ranges and needn't reach their ends.
Inputs may be any that keep to these rules, and one draw needn't show every extreme that they name: In each row the 4 lengths sum to 256, and the longest is exactly 192. Each row is a permutation of the 4 sequences of its group: seq_order[f, k] is the sequence placed k-th.
All inputs are finite; a program needn't handle non-finite values.
Results may differ from the reference program's by a relative error of at most 0.015.
Values may be sent and summed in bfloat16 or wider, within the bound.
No kernel may reach another device: no remote copies, remote signals or barrier semaphores. Data moves between devices by JAX's collectives and lax.ppermute only.
A program may use at most 192 MiB of HBM per device.

```python
import math
import jax
import jax.numpy as jnp
import numpy as np
from jax import lax

MODEL_WIDTH = 1024
QUERY_HEADS = 16
KEY_VALUE_HEADS = 8
HEAD_SIZE = 128
FF = 3072
TOK_DEV = 128
NSEQ_G = 4
LONGEST_LENGTH = 192
PACKED_TOKENS = 4096
N_FSDP = 16


def levels(key, shape, cuts, smallest, high):
    gain, own = 1.0, jax.random.fold_in(key, 6)
    for dim, blocks in cuts:
        heights = jnp.exp(jax.random.uniform(jax.random.fold_in(own, dim), (blocks,), jnp.float32, smallest / len(cuts), high / len(cuts)))
        gain = gain * jnp.repeat(heights, shape[dim] // blocks).reshape([-1 if axis == dim else 1 for axis in range(len(shape))])
    return gain


def profile(count, total, limit, lean):
    portions = [(1 << 20) // math.isqrt(rank ** lean) + 1 for rank in range(2, count + 1)]
    spare, counts = total - limit - (count - 1), [1] * (count - 1)
    while spare > 0:
        candidates = [i for i in range(count - 1) if counts[i] < limit]
        pool, remaining = sum([portions[i] for i in candidates]), spare
        for i in candidates:
            more = min(limit - counts[i], max(1, remaining * portions[i] // pool), spare)
            counts[i] = counts[i] + more
            spare = spare - more
    return np.array([limit] + counts)


def ragged(own_key, count, total, limit, skew):
    if count == 2:
        one = jax.random.randint(own_key, (), max(1, total - limit), min(limit, total - 1) + 1)
        return jnp.stack([one, total - one])
    tallies = jnp.asarray(profile(count, total, limit, skew), jnp.int32)
    pairs = (count - 1) // 2
    donor, receiver = tallies[1:1 + 2 * pairs:2], tallies[2:2 + 2 * pairs:2]
    margin = jnp.minimum(donor - 1, limit - receiver)
    shifted = jax.random.randint(jax.random.fold_in(own_key, 1), (pairs,), 0, 1 << 20) % (margin + 1)
    tallies = tallies.at[1:1 + 2 * pairs:2].set(donor - shifted).at[2:2 + 2 * pairs:2].set(receiver + shifted)
    return tallies[jax.random.permutation(jax.random.fold_in(own_key, 2), count)]


def gaussian(own_key, dims, spread, bound, shards=(), held_as=jnp.bfloat16):
    values = spread * jax.random.normal(own_key, dims, jnp.float32)
    if shards:
        values = values * levels(own_key, dims, shards, -0.22, 0.18)
    return jnp.clip(values, -bound, bound).astype(held_as)


def setup_inputs(seed: int = 0) -> dict:
    splits = jax.random.split(jax.random.key(seed), 16)
    tokens = gaussian(splits[0], (PACKED_TOKENS, MODEL_WIDTH), 1.0, 6.0, ((0, 32),))
    norm_gain = jnp.clip(jnp.exp(math.log(2.0) - 1.3862944 * jax.random.uniform(splits[1], (MODEL_WIDTH,), jnp.float32) ** levels(splits[1], (MODEL_WIDTH,), ((0, 32),), -0.2, 0.2)), 0.5, 2.0).astype(jnp.bfloat16)
    w_query = gaussian(splits[2], (MODEL_WIDTH, QUERY_HEADS * HEAD_SIZE), MODEL_WIDTH ** -0.5, 0.1875, ((0, 32),))
    key_projection_weight = gaussian(splits[3], (MODEL_WIDTH, KEY_VALUE_HEADS * HEAD_SIZE), MODEL_WIDTH ** -0.5, 0.1875, ((0, 32),))
    value_projection_weight = gaussian(splits[4], (MODEL_WIDTH, KEY_VALUE_HEADS * HEAD_SIZE), MODEL_WIDTH ** -0.5, 0.1875, ((0, 32),))
    w_output = gaussian(splits[5], (QUERY_HEADS * HEAD_SIZE, MODEL_WIDTH), 32 ** -0.5, 1.0, ((0, 32),))
    query_gain = jnp.clip(jnp.exp(math.log(1.5) - 1.0986123 * jax.random.uniform(splits[6], (HEAD_SIZE,), jnp.float32) ** levels(splits[6], (HEAD_SIZE,), ((0, 32),), -0.2, 0.2)), 0.5, 1.5).astype(jnp.bfloat16)
    key_gain = jnp.clip(jnp.exp(math.log(1.5) - 1.0986123 * jax.random.uniform(splits[7], (HEAD_SIZE,), jnp.float32) ** levels(splits[7], (HEAD_SIZE,), ((0, 32),), -0.2, 0.2)), 0.5, 1.5).astype(jnp.bfloat16)
    mlp_gain = jnp.clip(jnp.exp(math.log(2.0) - 1.3862944 * jax.random.uniform(splits[8], (MODEL_WIDTH,), jnp.float32) ** levels(splits[8], (MODEL_WIDTH,), ((0, 32),), -0.2, 0.2)), 0.5, 2.0).astype(jnp.bfloat16)
    w_gate = gaussian(splits[9], (MODEL_WIDTH, FF), MODEL_WIDTH ** -0.5, 0.1875, ((0, 32),))
    w_up = gaussian(splits[10], (MODEL_WIDTH, FF), MODEL_WIDTH ** -0.5, 0.1875, ((0, 32),))
    w_down = gaussian(splits[11], (FF, MODEL_WIDTH), (FF // 4) ** -0.5, 0.21875, ((0, 32),))
    lengths = jax.vmap(lambda own: ragged(own, NSEQ_G, 2 * TOK_DEV, LONGEST_LENGTH, 2))(jax.random.split(splits[12], N_FSDP)).reshape((N_FSDP, NSEQ_G)).astype(jnp.int32)
    seq_order = jax.vmap(lambda own: jax.random.permutation(own, NSEQ_G))(jax.random.split(splits[13], N_FSDP)).reshape((N_FSDP, NSEQ_G)).astype(jnp.int32)
    cotangent = gaussian(splits[14], (PACKED_TOKENS, MODEL_WIDTH), 1.0, 6.0, ((0, 32),))
    return {"tokens": tokens, "norm_gain": norm_gain, "w_query": w_query, "key_projection_weight": key_projection_weight, "value_projection_weight": value_projection_weight, "w_output": w_output, "query_gain": query_gain, "key_gain": key_gain, "mlp_gain": mlp_gain, "w_gate": w_gate, "w_up": w_up, "w_down": w_down, "lengths": lengths, "seq_order": seq_order, "cotangent": cotangent}


EPS = 1e-06
THETA = 1000000.0
HIGH_PRECISION = lax.Precision.HIGHEST

@jax.custom_vjp
def lower_bound(v):
    return lax.optimization_barrier(v.astype(jnp.bfloat16)).astype(jnp.float32)

@jax.custom_vjp
def lower_pullback(v):
    return v

def low_keep(v):
    return (lower_bound(v), None)

def low_pass(kept, grad):
    return (grad,)

def back_keep(v):
    return (v, None)

def back_low(kept, grad):
    return (lower_bound(grad),)
lower_bound.defvjp(low_keep, low_pass)
lower_pullback.defvjp(back_keep, back_low)

def rms_norm(values, gain_vec):
    return values * lax.rsqrt(lax.optimization_barrier(jnp.mean(values * values, axis=-1, keepdims=True)) + EPS) * gain_vec

def rotate(values, positions):
    half_width = values.shape[-1] // 2
    frequency = jnp.power(THETA, -jnp.arange(half_width, dtype=jnp.float32) * (2.0 / values.shape[-1]))
    angles = positions.astype(jnp.float32)[:, None] * frequency[None, :]
    cosine = jnp.cos(angles)[:, None, :]
    sine_part = jnp.sin(angles)[:, None, :]
    first_half = values[..., :half_width]
    second_half = values[..., half_width:]
    return jnp.concatenate([first_half * cosine - second_half * sine_part, second_half * cosine + first_half * sine_part], axis=-1)

def seq_bounds(lengths, seq_order):
    seq_count = lengths.shape[-1]
    picked = seq_order[..., :, None] == jnp.arange(seq_count, dtype=jnp.int32)
    packed = lax.optimization_barrier(jnp.sum(jnp.where(picked, lengths[..., None, :], 0), axis=-1)).astype(jnp.int32)
    seq_ends = jnp.cumsum(packed, axis=-1).astype(jnp.int32)
    return (seq_ends - packed, seq_ends)

def row_starts(row_ids, seq_starts, seq_ends):
    inside = (seq_starts[None, :] <= row_ids[:, None]) & (row_ids[:, None] < seq_ends[None, :])
    return lax.optimization_barrier(jnp.sum(jnp.where(inside, seq_starts[None, :], 0), axis=1)).astype(jnp.int32)

def attention(lower_query, key_low, lower_value, first_rows):
    query_tile_block = 256
    sequence_groups = QUERY_HEADS // KEY_VALUE_HEADS
    score_scale = HEAD_SIZE ** (-0.5)
    leading_zeros = jnp.zeros((LONGEST_LENGTH, KEY_VALUE_HEADS, HEAD_SIZE), jnp.float32)
    key_padded = jnp.concatenate([leading_zeros, key_low], axis=0)
    value_padded = jnp.concatenate([leading_zeros, lower_value], axis=0)

    @jax.checkpoint
    def one_block(index):
        begin_offset = index * query_tile_block
        query_portion = lax.dynamic_slice_in_dim(lower_query, begin_offset, query_tile_block, 0).reshape(query_tile_block, KEY_VALUE_HEADS, sequence_groups, HEAD_SIZE)
        key_part = lax.dynamic_slice_in_dim(key_padded, begin_offset, query_tile_block + LONGEST_LENGTH, 0)
        value_part = lax.dynamic_slice_in_dim(value_padded, begin_offset, query_tile_block + LONGEST_LENGTH, 0)
        starts_part = lax.dynamic_slice_in_dim(first_rows, begin_offset, query_tile_block, 0)
        row_ids = begin_offset + jnp.arange(query_tile_block, dtype=jnp.int32)
        col_ids = begin_offset - LONGEST_LENGTH + jnp.arange(query_tile_block + LONGEST_LENGTH, dtype=jnp.int32)
        allowed = (col_ids[None, :] <= row_ids[:, None]) & (col_ids[None, :] >= starts_part[:, None])
        scores = lower_pullback(jnp.einsum('qhgd,khd->hgqk', query_portion, key_part, precision=HIGH_PRECISION) * score_scale)
        scores = jnp.where(allowed[None, None], scores, -1e+30)
        row_max = lax.optimization_barrier(jnp.max(scores, axis=-1, keepdims=True))
        exp_scores = jnp.exp(scores - row_max)
        attn_probs = exp_scores / lax.optimization_barrier(jnp.sum(exp_scores, axis=-1, keepdims=True))
        head_mix = jnp.einsum('hgqk,khd->qhgd', lower_bound(attn_probs), value_part, precision=HIGH_PRECISION)
        return head_mix.reshape(query_tile_block, QUERY_HEADS * HEAD_SIZE)
    blocks = lax.map(one_block, jnp.arange(PACKED_TOKENS // query_tile_block, dtype=jnp.int32))
    return blocks.reshape(PACKED_TOKENS, QUERY_HEADS * HEAD_SIZE)

def forward(inputs, gain_first, query_w, key_matrix, value_matrix, output_w, query_norm, key_norm, gain_second, gate_w, up_w, down_w, positions, first_rows):
    normalized_input = lower_bound(rms_norm(inputs, gain_first))
    query_raw = lower_pullback(jnp.dot(normalized_input, query_w, precision=HIGH_PRECISION)).reshape(PACKED_TOKENS, QUERY_HEADS, HEAD_SIZE)
    unnormed_key = lower_pullback(jnp.dot(normalized_input, key_matrix, precision=HIGH_PRECISION)).reshape(PACKED_TOKENS, KEY_VALUE_HEADS, HEAD_SIZE)
    lower_value = lower_bound(lower_pullback(jnp.dot(normalized_input, value_matrix, precision=HIGH_PRECISION))).reshape(PACKED_TOKENS, KEY_VALUE_HEADS, HEAD_SIZE)
    lower_query = lower_bound(rotate(rms_norm(query_raw, query_norm), positions))
    key_low = lower_bound(rotate(rms_norm(unnormed_key, key_norm), positions))
    attn_low = lower_bound(lower_pullback(attention(lower_query, key_low, lower_value, first_rows)))
    hidden = inputs + lower_pullback(jnp.dot(attn_low, output_w, precision=HIGH_PRECISION))
    normed_mid = lower_bound(rms_norm(hidden, gain_second))
    gate_pre = lower_pullback(jnp.dot(normed_mid, gate_w, precision=HIGH_PRECISION))
    upward = lower_pullback(jnp.dot(normed_mid, up_w, precision=HIGH_PRECISION))
    mixed_low = lower_bound(gate_pre / (1.0 + jnp.exp(-gate_pre)) * upward)
    return hidden + lower_pullback(jnp.dot(mixed_low, down_w, precision=HIGH_PRECISION))

def reference(tokens, norm_gain, w_query, key_projection_weight, value_projection_weight, w_output, query_gain, key_gain, mlp_gain, w_gate, w_up, w_down, lengths, seq_order, cotangent):
    local_starts, local_ends = seq_bounds(lengths, seq_order)
    group_offsets = (jnp.arange(N_FSDP, dtype=jnp.int32) * (2 * TOK_DEV))[:, None]
    seq_starts = (local_starts + group_offsets).reshape(-1).astype(jnp.int32)
    seq_ends = (local_ends + group_offsets).reshape(-1).astype(jnp.int32)
    row_ids = jnp.arange(PACKED_TOKENS, dtype=jnp.int32)
    first_rows = row_starts(row_ids, seq_starts, seq_ends)
    positions = row_ids - first_rows
    params = tuple((weight_arg.astype(jnp.float32) for weight_arg in (norm_gain, w_query, key_projection_weight, value_projection_weight, w_output, query_gain, key_gain, mlp_gain, w_gate, w_up, w_down)))

    def whole(inputs, *weights):
        return forward(inputs, *weights, positions, first_rows)
    result, pull_back = jax.vjp(whole, tokens.astype(jnp.float32), *params)
    gradients = pull_back(cotangent.astype(jnp.float32))
    return (result.astype(jnp.bfloat16), gradients[0], gradients[1], gradients[2], gradients[3], gradients[4], gradients[5], gradients[6], gradients[7], gradients[8], gradients[9], gradients[10], gradients[11])
```

```python
import jax
import jax.numpy as jnp
import numpy as np
from jax import lax
from jax.sharding import Mesh, PartitionSpec as P

QUERY_HEADS = 16
KEY_VALUE_HEADS = 8
HEAD_SIZE = 128
GROUP = QUERY_HEADS // KEY_VALUE_HEADS

EPS = 1e-06
THETA = 1000000.0
SCALE = HEAD_SIZE ** (-0.5)

ALL = ("data", "x", "core", "seq")
BF = jnp.bfloat16
F32 = jnp.float32
SWAP = [(0, 1), (1, 0)]


def mm(a, b):
    return jnp.dot(a, b, preferred_element_type=F32)


def mm_nt(a, b):
    return lax.dot_general(a, b, (((1,), (1,)), ((), ())), preferred_element_type=F32)


def mm_tn(a, b):
    return lax.dot_general(a, b, (((0,), (0,)), ((), ())), preferred_element_type=F32)


def flip(value, axis):
    return lax.ppermute(value, axis, SWAP)


def after(value, *others):
    return lax.optimization_barrier((value,) + others)[0]


def gather_plane(block):
    from_d = lax.ppermute(block, ("x", "seq"), [(i, i ^ 3) for i in range(4)])
    near = jnp.stack([block, flip(block, "seq"), flip(block, "x"), from_d])
    return jnp.concatenate([near, flip(near, "core")], axis=0)


def scatter_plane(parts):
    total = parts[:4] + flip(parts[4:].astype(BF), "core").astype(F32)
    low = total[1:].astype(BF)
    from_d = lax.ppermute(low[2], ("x", "seq"), [(i, i ^ 3) for i in range(4)])
    from_y = flip(low[0], "seq")
    from_x = flip(low[1], "x")
    return total[0] + from_y.astype(F32) + from_x.astype(F32) + from_d.astype(F32)


def to_all(payload):
    return lax.all_to_all(payload, ALL, split_axis=0, concat_axis=0, tiled=True)


def row_routes(count, shift):
    return [
        (count * j + (d + shift) % count, d * 8 + j) for d in range(count) for j in range(8)
    ]


def gather_rows(block, count, mine):
    parts = [lax.ppermute(block, ALL, row_routes(count, s)) for s in range(count)]
    both = jnp.stack(parts + parts)
    start = (count - mine) % count
    turned = lax.dynamic_slice_in_dim(both, start, count, 0)
    return turned.reshape(count * block.shape[0], block.shape[1])


def scatter_rows(grad, count, mine):
    parts = grad.reshape(count, grad.shape[0] // count, grad.shape[1])
    both = jnp.concatenate([parts, parts], axis=0)
    turned = lax.dynamic_slice_in_dim(both, mine, count, 0)
    total = 0.0
    for s in range(count):
        back = [(b, a) for a, b in row_routes(count, s)]
        total = total + lax.ppermute(turned[s], ALL, back).astype(F32)
    return total


def col_payload(weights, extra=None):
    rows = weights[0].shape[0]
    pieces = []
    for weight in weights:
        per = weight.shape[1] // (8 * 128)
        cut = weight.reshape(rows, 8, per, 128).transpose(1, 2, 0, 3)
        pieces.append(cut.reshape(8, per * rows, 128))
    if extra is not None:
        pieces.append(jnp.broadcast_to(extra[None], (8,) + extra.shape))
    return jnp.concatenate(pieces, axis=1)


def send_cols(weights, count, extra=None):
    payload = col_payload(weights, extra)
    payload = jnp.broadcast_to(payload[None], (count,) + payload.shape)
    return to_all(payload.reshape((count * 8,) + payload.shape[2:]))


def cols_of(received, rows, blocks):
    devices = received.shape[0]
    return jnp.concatenate(
        [
            received[:, c * rows : (c + 1) * rows].reshape(devices * rows, 128)
            for c in range(blocks)
        ],
        axis=1,
    )


def grad_payload(grad, devices, extra=None):
    rows = grad.shape[0] // devices
    blocks = grad.shape[1] // 128
    cut = [grad[:, c * 128 : (c + 1) * 128].reshape(devices, rows, 128) for c in range(blocks)]
    if extra is not None:
        cut.append(jnp.broadcast_to(extra[None], (devices,) + extra.shape))
    return jnp.concatenate(cut, axis=1)


def grad_cols(total, rows, first, per):
    part = total[:, first * rows : (first + per) * rows].reshape(8, per, rows, 128)
    return part.transpose(2, 0, 1, 3).reshape(rows, 8 * per * 128)


def inv_rms(values):
    return lax.rsqrt(jnp.mean(values * values, axis=-1, keepdims=True) + EPS)


def turn(values, cosine, sine):
    half = values.shape[-1] // 2
    a, b = values[..., :half], values[..., half:]
    return jnp.concatenate([a * cosine - b * sine, b * cosine + a * sine], axis=-1)


def head_path(raw, gain, cosine, sine):
    return turn(raw * inv_rms(raw) * gain, cosine, sine).astype(BF)


def head_pull(grad, raw, gain, cosine, sine):
    back = turn(grad, cosine, -sine)
    r = inv_rms(raw)
    u = back * gain
    grad_gain = jnp.sum(back * raw * r, axis=(0, 1))
    return r * u - raw * (r * r * r) * jnp.mean(u * raw, axis=-1, keepdims=True), grad_gain


def seq_bounds(lengths, seq_order):
    seq_count = lengths.shape[-1]
    picked = seq_order[..., :, None] == jnp.arange(seq_count, dtype=jnp.int32)
    packed = jnp.sum(jnp.where(picked, lengths[..., None, :], 0), axis=-1)
    seq_ends = jnp.cumsum(packed, axis=-1)
    return (seq_ends - packed, seq_ends)


def local(
    tokens,
    norm_gain,
    w_query,
    w_key,
    w_value,
    w_output,
    query_gain,
    key_gain,
    mlp_gain,
    w_gate,
    w_up,
    w_down,
    lengths,
    seq_order,
    cotangent,
):
    rows, width = tokens.shape
    count = lax.axis_size("data")
    devices = count * 8
    mine = lax.axis_index("data")
    in_seq = lax.axis_index("seq")
    w_rows = w_query.shape[0]
    gains = query_gain.shape[0]
    n_seq = lengths.shape[1]

    extra = jnp.stack([query_gain, key_gain]).reshape(1, 2 * gains)
    extra = jnp.concatenate([extra, norm_gain[None], mlp_gain[None]], axis=1)
    n_extra = extra.shape[1]
    extra = jnp.pad(extra, ((0, 7), (0, 128 - n_extra)))
    got_qkv = send_cols([w_query, w_key, w_value], count, extra)
    qkv_full = cols_of(got_qkv, w_rows, 4)
    got_gains = got_qkv[:, 4 * w_rows, :n_extra].astype(F32)
    query_norm = got_gains[:, :gains].reshape(-1)
    key_norm = got_gains[:, gains : 2 * gains].reshape(-1)
    gain_in = got_gains[:, 2 * gains : 2 * gains + w_rows].reshape(-1)
    gain_mid = got_gains[:, 2 * gains + w_rows :].reshape(-1)
    got_gu = send_cols([after(w_gate, got_qkv), w_up], count)
    gu_full = cols_of(got_gu, w_rows, got_gu.shape[1] // w_rows)

    marks = jnp.concatenate([lengths, seq_order], axis=1).astype(BF)
    marks = jnp.pad(marks, ((0, 7), (0, width - 2 * n_seq)))
    got_tokens = gather_plane(jnp.concatenate([tokens, marks], axis=0))
    plane_rows = 8 * rows
    inputs = got_tokens[:, :rows].reshape(plane_rows, width).astype(F32)
    marks = got_tokens[0::2, rows, : 2 * n_seq].astype(jnp.int32)
    starts, ends = seq_bounds(marks[:, :n_seq], marks[:, n_seq:])
    row_ids = jnp.arange(rows, dtype=jnp.int32)
    row_ids = jnp.concatenate([in_seq * rows + row_ids, (1 - in_seq) * rows + row_ids])
    inside = (starts[:, None, :] <= row_ids[None, :, None]) & (
        row_ids[None, :, None] < ends[:, None, :]
    )
    first_rows = jnp.sum(jnp.where(inside, starts[:, None, :], 0), axis=2)
    allowed = (row_ids[None, None, :] <= row_ids[None, :, None]) & (
        row_ids[None, None, :] >= first_rows[:, :, None]
    )
    positions = (row_ids[None, :] - first_rows).reshape(plane_rows)
    half = HEAD_SIZE // 2
    frequency = jnp.power(THETA, -jnp.arange(half, dtype=F32) * (2.0 / HEAD_SIZE))
    angles = positions.astype(F32)[:, None] * frequency[None, :]
    cosine = jnp.cos(angles)[:, None, :]
    sine = jnp.sin(angles)[:, None, :]

    out_full = gather_rows(after(w_output, got_tokens), count, mine)
    cot_all = gather_plane(after(cotangent, got_tokens)).reshape(plane_rows, width)
    down_full = gather_rows(after(w_down, out_full), count, mine)
    ff = down_full.shape[0]
    normed_in = (inputs * inv_rms(inputs) * gain_in).astype(BF)
    qkv = mm(normed_in, qkv_full)
    query_raw = qkv[:, : GROUP * HEAD_SIZE].reshape(plane_rows, GROUP, HEAD_SIZE)
    key_raw = qkv[:, GROUP * HEAD_SIZE : -HEAD_SIZE].reshape(plane_rows, 1, HEAD_SIZE)
    span = 2 * rows
    query_low = head_path(query_raw, query_norm, cosine, sine).reshape(4, span, GROUP, HEAD_SIZE)
    key_low = head_path(key_raw, key_norm, cosine, sine).reshape(4, span, HEAD_SIZE)
    value_low = qkv[:, -HEAD_SIZE:].astype(BF).reshape(4, span, HEAD_SIZE)
    scores = jnp.einsum("bqhd,bkd->bhqk", query_low, key_low, preferred_element_type=F32) * SCALE
    scores = jnp.where(allowed[:, None], scores, -1e30)
    exp_scores = jnp.exp(scores - jnp.max(scores, axis=-1, keepdims=True))
    probs = exp_scores / jnp.sum(exp_scores, axis=-1, keepdims=True)
    probs_low = probs.astype(BF)
    attn_low = (
        jnp.einsum("bhqk,bkd->bqhd", probs_low, value_low, preferred_element_type=F32)
        .astype(BF)
        .reshape(plane_rows, GROUP * HEAD_SIZE)
    )
    out_parts = mm(attn_low, out_full).reshape(8, rows, width)
    hidden = tokens.astype(F32) + scatter_plane(out_parts)

    r_mid = inv_rms(hidden)
    normed_mid = gather_plane((hidden * r_mid * gain_mid).astype(BF)).reshape(plane_rows, width)
    gate_up = mm(normed_mid, gu_full)
    gate_pre, upward = gate_up[:, :ff], gate_up[:, ff:]
    sigma = 1.0 / (1.0 + jnp.exp(-gate_pre))
    silu = gate_pre * sigma
    mixed_low = (silu * upward).astype(BF)
    grad_mixed = mm_nt(cot_all, down_full)
    grad_gate = grad_mixed * upward * sigma * (1.0 + gate_pre * (1.0 - sigma))
    grad_up = grad_mixed * silu
    grad_gu = jnp.concatenate([grad_gate.astype(BF), grad_up.astype(BF)], axis=1)
    u_mid = gain_mid * scatter_plane(mm_nt(grad_gu, gu_full).reshape(8, rows, width))
    cot = cotangent.astype(F32)
    grad_hidden = (
        cot
        + r_mid * u_mid
        - hidden * (r_mid * r_mid * r_mid) * jnp.mean(u_mid * hidden, axis=-1, keepdims=True)
    )
    grad_out_all = gather_plane(grad_hidden.astype(BF)).reshape(plane_rows, width)

    result_parts = mm(mixed_low, down_full).reshape(8, rows, width)
    result = (hidden + scatter_plane(result_parts)).astype(BF)
    got_down = scatter_rows(mm_tn(mixed_low, cot_all).astype(BF), count, mine)
    got_ggu = to_all(grad_payload(mm_tn(normed_mid, grad_gu).astype(BF), devices))

    got_out = scatter_rows(mm_tn(attn_low, grad_out_all).astype(BF), count, mine)
    grad_attn = mm_nt(grad_out_all, out_full).astype(BF).reshape(4, span, GROUP, HEAD_SIZE)
    grad_probs = jnp.einsum("bqhd,bkd->bhqk", grad_attn, value_low, preferred_element_type=F32)
    row_dot = jnp.sum(probs * grad_probs, axis=-1, keepdims=True)
    grad_scores = (probs * (grad_probs - row_dot)).astype(BF)
    grad_query = (
        jnp.einsum("bhqk,bkd->bqhd", grad_scores, key_low, preferred_element_type=F32) * SCALE
    )
    grad_key = (
        jnp.einsum("bhqk,bqhd->bkd", grad_scores, query_low, preferred_element_type=F32) * SCALE
    )
    grad_value = jnp.einsum("bhqk,bqhd->bkd", probs_low, grad_attn, preferred_element_type=F32)
    grad_query_raw, query_gain_part = head_pull(
        grad_query.reshape(plane_rows, GROUP, HEAD_SIZE), query_raw, query_norm, cosine, sine
    )
    grad_key_raw, key_gain_part = head_pull(
        grad_key.reshape(plane_rows, 1, HEAD_SIZE), key_raw, key_norm, cosine, sine
    )
    grad_qkv = jnp.concatenate(
        [
            grad_query_raw.reshape(plane_rows, GROUP * HEAD_SIZE),
            grad_key_raw.reshape(plane_rows, HEAD_SIZE),
            grad_value.reshape(plane_rows, HEAD_SIZE),
        ],
        axis=1,
    ).astype(BF)
    gain_parts = jnp.stack([query_gain_part, key_gain_part])
    gain_high = gain_parts.astype(BF)
    gain_low = (gain_parts - gain_high.astype(F32)).astype(BF)
    gain_rows = jnp.pad(jnp.concatenate([gain_high, gain_low]), ((0, 4), (0, 0)))
    got_gqkv = to_all(
        grad_payload(mm_tn(normed_in, grad_qkv).astype(BF), devices, gain_rows)
    )
    u_in = gain_in * scatter_plane(mm_nt(grad_qkv, qkv_full).reshape(8, rows, width))
    x = tokens.astype(F32)
    r_in = inv_rms(x)
    grad_tokens = (
        grad_hidden
        + r_in * u_in
        - x * (r_in * r_in * r_in) * jnp.mean(u_in * x, axis=-1, keepdims=True)
    )

    def owned(got):
        return jnp.sum(got.reshape((count, 8) + got.shape[1:]).astype(F32), axis=0)

    def of_weight(total, first, weight):
        per = weight.shape[1] // (8 * 128)
        plain = grad_cols(total, w_rows, first, per)
        return plain, jnp.sum(plain * weight.astype(F32), axis=1)

    total_qkv = owned(got_gqkv)
    grad_w_query, gain_q = of_weight(total_qkv, 0, w_query)
    grad_w_key, gain_k = of_weight(total_qkv, 2, w_key)
    grad_w_value, gain_v = of_weight(total_qkv, 3, w_value)
    total_gu = owned(got_ggu)
    grad_w_gate, gain_g = of_weight(total_gu, 0, w_gate)
    grad_w_up, gain_u = of_weight(total_gu, ff // 128, w_up)
    gain_sums = jnp.sum(total_qkv[:, 4 * w_rows :], axis=0)
    me = lax.axis_index(ALL)
    gain_sums = gain_sums[0:2] + gain_sums[2:4]
    gain_mine = lax.dynamic_slice_in_dim(gain_sums, me * gains, gains, 1)
    return (
        result,
        grad_tokens,
        (gain_q + gain_k + gain_v) / norm_gain.astype(F32),
        grad_w_query,
        grad_w_key,
        grad_w_value,
        got_out,
        gain_mine[0],
        gain_mine[1],
        (gain_g + gain_u) / mlp_gain.astype(F32),
        grad_w_gate,
        grad_w_up,
        got_down,
    )


def solution(mesh):
    fsdp, seq = mesh.shape["fsdp"], mesh.shape["seq"]
    fine = Mesh(np.asarray(mesh.devices).reshape(fsdp // 4, 2, 2, seq), ALL)
    matrix, vector, group = P(ALL, None), P(ALL), P(ALL[:3], None)
    placed = (
        matrix, vector, matrix, matrix, matrix, matrix, vector, vector, vector,
        matrix, matrix, matrix, group, group, matrix,
    )
    outs = (
        matrix, matrix, vector, matrix, matrix, matrix, matrix, vector, vector, vector,
        matrix, matrix, matrix,
    )
    return jax.shard_map(local, mesh=fine, in_specs=placed, out_specs=outs, check_vma=False)
```

```python
import functools

import jax
import jax.numpy as jnp
import numpy as np
from jax import lax
from jax.experimental import pallas as pl
from jax.experimental.pallas import tpu as pltpu
from jax.sharding import Mesh, PartitionSpec as P

QUERY_HEADS = 16
KEY_VALUE_HEADS = 8
HEAD_SIZE = 128
GROUP = QUERY_HEADS // KEY_VALUE_HEADS
HEADS_WIDTH = GROUP * HEAD_SIZE

EPS = 1e-06
THETA = 1000000.0
SCALE = HEAD_SIZE ** (-0.5)
EXTRA_ROWS = 16

ALL = ("data", "x", "core", "seq")
BF = jnp.bfloat16
F32 = jnp.float32
SWAP = [(0, 1), (1, 0)]


def mm(a, b):
    return lax.dot_general(a, b, (((1,), (0,)), ((), ())), preferred_element_type=F32)


def mm_nt(a, b):
    return lax.dot_general(a, b, (((1,), (1,)), ((), ())), preferred_element_type=F32)


def mm_tn(a, b):
    return lax.dot_general(a, b, (((0,), (0,)), ((), ())), preferred_element_type=F32)


def together(*values):
    return lax.optimization_barrier(values)


def flip(value, axis):
    return lax.ppermute(value, axis, SWAP)


def flip_diagonal(value):
    return lax.ppermute(value, ("x", "seq"), [(i, i ^ 3) for i in range(4)])


def gather_chips(block):
    from_d = flip_diagonal(block)
    return jnp.stack([block, flip(block, "seq"), flip(block, "x"), from_d])


def exchange(own, to_y, to_x, to_d):
    from_d = flip_diagonal(to_d)
    return own, flip(to_y, "seq"), flip(to_x, "x"), from_d


def in_plane_all(payload):
    return lax.all_to_all(payload, ALL[1:], split_axis=0, concat_axis=0, tiled=True)


def to_row_place(block, count):
    route = [(count * j + d, d * 8 + j) for d in range(count) for j in range(8)]
    return lax.ppermute(block, ALL, route)


def doubling_orders(count):
    orders, bit = [[0]], count // 2
    while bit:
        orders.append([o ^ bit for order in orders for o in order])
        bit //= 2
    return orders


def across(value, bit):
    return lax.ppermute(value, "data", [(d, d ^ bit) for d in range(lax.axis_size("data"))])


def double(arrays, last=False):
    arrays, bit = list(arrays), lax.axis_size("data") // 2
    while bit > 1 and not last:
        arrays.append(across(jnp.concatenate(arrays), bit))
        bit //= 2
    if last:
        arrays.append(across(jnp.concatenate(arrays), 1))
    return arrays


def plane_sum(value, *axes):
    for axis in axes or ("core", "x", "seq"):
        value = value + flip(value, axis)
    return value


def data_sum(value, last=False):
    bit = lax.axis_size("data") // 2
    while bit > 1 and not last:
        value = value + across(value, bit)
        bit //= 2
    return value + across(value, 1) if last else value


def to_row_owner(block, count):
    route = [(d * 8 + j, count * j + d) for d in range(count) for j in range(8)]
    return lax.ppermute(block, ALL, route)


def spec(kind, shape, at):
    zeros = (0,) * (len(shape) - 1)
    if kind == "blocks":
        return pl.BlockSpec((2,) + shape[1:], lambda g: (g,) + zeros)
    if kind == "half":
        return pl.BlockSpec((shape[0] // 2,) + shape[1:], lambda g: (g,) + zeros)
    if kind == "group":
        return pl.BlockSpec((shape[0] // 4,) + shape[1:], lambda g: (at + g,) + zeros)
    if kind == "scalars":
        return pl.BlockSpec(memory_space=pltpu.SMEM)
    if kind == "kept":
        return pl.BlockSpec(memory_space=pl.ANY)
    return pl.BlockSpec(shape, lambda g: (0,) + zeros)


def call_half(kernel, which, outs, args, kept=(), scratch=()):
    at = 2 * which
    given = list(args) + [("kept", array) for array in kept]
    aliases = {len(args) + k: k for k in range(len(kept))}
    n_args = len(args)

    def body(*refs):
        kernel(*refs[:n_args], *refs[n_args + len(kept) :])

    return pl.pallas_call(
        body,
        grid=(2,),
        out_shape=tuple(jax.ShapeDtypeStruct(shape, dtype) for _, shape, dtype in outs),
        in_specs=[spec(kind, arg.shape, at) for kind, arg in given],
        out_specs=tuple(spec(kind, shape, at) for kind, shape, _ in outs),
        scratch_shapes=list(scratch),
        input_output_aliases=aliases,
        compiler_params=pltpu.CompilerParams(
            vmem_limit_bytes=24 * 2**20, dimension_semantics=("arbitrary",)
        ),
    )(*[arg for _, arg in given])


def call(kernel, outs, *args):
    vmem = pl.BlockSpec(memory_space=pltpu.VMEM)
    return pl.pallas_call(
        kernel,
        out_shape=tuple(jax.ShapeDtypeStruct(shape, dtype) for shape, dtype in outs),
        in_specs=[vmem for _ in args],
        out_specs=tuple(vmem for _ in outs),
        compiler_params=pltpu.CompilerParams(vmem_limit_bytes=12 * 2**20),
    )(*args)


def whole(*arrays):
    return [("whole", array) for array in arrays]


def pack_kernel(widths, *refs):
    *weights, out = refs
    for j in range(8):
        at = 0
        for width, ref in zip(widths, weights):
            out[j, :, at : at + width] = ref[:, j * width : (j + 1) * width]
            at += width


def pack(*weights):
    widths = [w.shape[1] // 8 for w in weights]
    shape = (8, weights[0].shape[0], sum(widths))
    return pl.pallas_call(
        functools.partial(pack_kernel, widths),
        grid=(1,),
        out_shape=jax.ShapeDtypeStruct(shape, BF),
        in_specs=[spec("whole", w.shape, 0) for w in weights],
        out_specs=spec("whole", shape, 0),
    )(*weights)


def copy_kernel(tokens, payload, out):
    out[...] = tokens[...]


def ordered_after(tokens, payload):
    vmem = pl.BlockSpec(memory_space=pltpu.VMEM)
    return pl.pallas_call(
        copy_kernel,
        out_shape=jax.ShapeDtypeStruct(tokens.shape, tokens.dtype),
        in_specs=[vmem, pl.BlockSpec(memory_space=pl.ANY)],
        out_specs=vmem,
    )(tokens, payload)


def marks_kernel(scalars, norm_gain, mlp_gain, query_gain, key_gain, lengths, seq_order, out):
    width = out.shape[1]

    def placed(ref, at):
        line = ref[...].astype(F32)
        line = jnp.concatenate([line, jnp.zeros((1, width - line.shape[1]), F32)], axis=1)
        return pltpu.roll(line, at * ref.shape[1], 1)

    lines = [placed(ref, scalars[2]) for ref in (norm_gain, mlp_gain, query_gain, key_gain)]
    once = (1 - scalars[1]).astype(F32)
    lines += [placed(ref, scalars[2] // 2) * once for ref in (lengths, seq_order)]
    lines.append(jnp.zeros((2, width), F32))
    out[...] = jnp.concatenate(lines, axis=0).astype(BF)


def make_marks(scalars, width, *values):
    vmem = pl.BlockSpec(memory_space=pltpu.VMEM)
    return pl.pallas_call(
        marks_kernel,
        out_shape=jax.ShapeDtypeStruct((8, width), BF),
        in_specs=[pl.BlockSpec(memory_space=pltpu.SMEM)] + [vmem for _ in values],
        out_specs=vmem,
    )(scalars, *values)


def setup_kernel(n_seq, scalars, marks, gain_in, gain_mid, head_gains, starts):
    rows = marks[...].astype(F32)
    gain_in[...] = rows[0:1]
    gain_mid[...] = rows[1:2]
    head_gains[...] = rows[2:4, :HEAD_SIZE]
    width = rows.shape[1]
    lane = lax.broadcasted_iota(jnp.int32, (1, 128), 1).astype(F32)
    for k, relative in enumerate((0, 2, 1, 3)):
        back = width - lax.bitwise_xor(scalars[2] // 2, relative) * n_seq
        lengths, order = [pltpu.roll(rows[q : q + 1], back, 1)[:, :128] for q in (4, 5)]
        at = jnp.zeros((1, 1), F32)
        for q in range(n_seq):
            starts[k, q : q + 1, :] = jnp.broadcast_to(at, (1, 128))
            mine = (lane == order[:, q : q + 1]) & (lane < n_seq)
            at = at + jnp.sum(jnp.where(mine, lengths, 0.0), axis=1, keepdims=True)
        starts[k, n_seq:, :] = jnp.full((8 - n_seq, 128), 1e9, F32)


def setup(scalars, marks, n_seq):
    width = marks.shape[1]
    outs = [((1, width), F32), ((1, width), F32), ((2, HEAD_SIZE), F32), ((4, 8, 128), F32)]
    vmem = pl.BlockSpec(memory_space=pltpu.VMEM)
    return pl.pallas_call(
        functools.partial(setup_kernel, n_seq),
        out_shape=tuple(jax.ShapeDtypeStruct(shape, dtype) for shape, dtype in outs),
        in_specs=[pl.BlockSpec(memory_space=pltpu.SMEM), vmem],
        out_specs=tuple(vmem for _ in outs),
    )(scalars, marks)


def assemble_kernel(orders, cuts, scalars, *refs):
    arrays, outs = refs[: len(orders)], refs[len(orders) :]
    for order, ref in zip(orders, arrays):
        for k, relative in enumerate(order):
            place, start = lax.bitwise_xor(scalars[0], relative), 0
            for size, out in zip(cuts, outs):
                at = pl.multiple_of(place * size, size)
                out[pl.ds(at, size), :] = ref[k, start : start + size, :]
                start += size


def assemble(arrays, scalars, *cuts):
    count = sum(array.shape[0] for array in arrays)
    orders = doubling_orders(count)
    _, size, width = arrays[0].shape
    cuts = cuts or (size,)
    if any(cut % 16 for cut in cuts):
        came = jnp.concatenate(arrays)
        at = jnp.asarray(np.argsort([o for order in orders for o in order]))
        came = came[at[jnp.arange(count) ^ scalars[0]]]
        ends = np.cumsum(cuts)
        return [came[:, b - a : b].reshape(count * a, width) for a, b in zip(cuts, ends)]
    vmem = pl.BlockSpec(memory_space=pltpu.VMEM)
    return pl.pallas_call(
        functools.partial(assemble_kernel, orders, cuts),
        out_shape=tuple(jax.ShapeDtypeStruct((count * cut, width), BF) for cut in cuts),
        in_specs=[pl.BlockSpec(memory_space=pltpu.SMEM)] + [vmem for _ in arrays],
        out_specs=tuple(vmem for _ in cuts),
    )(scalars, *arrays)


def unpack_kernel(widths, start, got, gain, *refs):
    weights, outs, gain_out = refs[: len(widths)], refs[len(widths) : -1], refs[-1]
    sums = 0.0
    for j in range(8):
        at = start
        for width, weight, out in zip(widths, weights, outs):
            piece = got[j, :, at : at + width].astype(F32)
            out[:, j * width : (j + 1) * width] = piece
            kept = weight[:, j * width : (j + 1) * width].astype(F32)
            sums = sums + jnp.sum(piece * kept, axis=1, keepdims=True)
            at += width
    gain_out[...] = sums / gain[...]


def unpack(got, start, gain, *weights):
    widths = [w.shape[1] // 8 for w in weights]
    outs = [(w.shape, F32) for w in weights] + [((gain.shape[0], 1), F32)]
    *grads, gain_grad = call(
        functools.partial(unpack_kernel, widths, start),
        outs,
        got,
        gain.astype(F32)[:, None],
        *weights,
    )
    return grads, gain_grad[:, 0]


def merge_kernel(near, other, own, to_y, to_x, to_d):
    own[...] = near[0] + other[0].astype(F32)
    for k, out in ((1, to_y), (2, to_x), (3, to_d)):
        out[...] = (near[k] + other[k].astype(F32)).astype(BF)


def merge(near, other):
    shape = near.shape[1:]
    return call(merge_kernel, [(shape, F32)] + [(shape, BF)] * 3, near, other)


def inv_rms(values):
    return lax.rsqrt(jnp.mean(values * values, axis=-1, keepdims=True) + EPS)


def summed(own, from_y, from_x, from_d, rows):
    total = own[:rows]
    for ref in (from_y, from_x, from_d):
        total = total + ref[:rows].astype(F32)
    return total


def hidden_kernel(tokens, own, from_y, from_x, from_d, gain, hidden, normed):
    total = tokens[...].astype(F32) + summed(own, from_y, from_x, from_d, tokens.shape[0])
    hidden[...] = total
    normed[...] = (total * inv_rms(total) * gain[...]).astype(BF)


def result_kernel(hidden, own, from_y, from_x, from_d, result):
    total = hidden[...] + summed(own, from_y, from_x, from_d, hidden.shape[0])
    result[...] = total.astype(BF)


def norm_pull_kernel(values, base, own, from_y, from_x, from_d, gain, out, *low):
    v = values[...].astype(F32)
    u = summed(own, from_y, from_x, from_d, v.shape[0]) * gain[...]
    r = inv_rms(v)
    total = base[...].astype(F32) + r * u - v * (r * r * r) * jnp.mean(u * v, -1, keepdims=True)
    out[...] = total
    for ref in low:
        ref[...] = total.astype(BF)


def turn(values, cosine, sine):
    return values * cosine + pltpu.roll(values, HEAD_SIZE // 2, 1) * sine


def turned_mask(starts, in_seq, rows):
    span = 2 * rows

    def ids(dim):
        shape = (span, 1) if dim == 0 else (1, span)
        at = lax.broadcasted_iota(jnp.int32, shape, dim)
        return lax.rem(at + in_seq * rows, span).astype(F32)

    def of_sequence(row_ids):
        return sum((row_ids >= starts[0, k : k + 1, 0:1]).astype(F32) for k in range(8))

    down, along = ids(0), ids(1)
    allowed = (along <= down) & (of_sequence(along) == of_sequence(down))
    return jnp.where(allowed, 0.0, -1e30).astype(F32)


def softmax(query, key, bias):
    scores = mm_nt(query, key) * SCALE + bias
    exp_scores = jnp.exp(scores - jnp.max(scores, axis=-1, keepdims=True))
    return exp_scores / jnp.sum(exp_scores, axis=-1, keepdims=True)


def group_of(blocks, start, rows):
    return jnp.concatenate([blocks[0, start : start + rows, :], blocks[1, start : start + rows, :]])


def split_out(product, rows, parts):
    for k in range(2):
        parts[k, :rows, :] = product[k * rows : (k + 1) * rows].astype(parts.dtype)


def attend_kernel(
    rows, scalars, starts, blocks, weight, gain, head_gains, cosine, sine, *outs
):
    normed, raw, low, attn = outs
    x = group_of(blocks, 0, rows).astype(F32)
    x = (x * inv_rms(x) * gain[...]).astype(BF)
    normed[...] = x
    qkv = mm(x, weight[...])
    raw[...] = qkv[:, : HEADS_WIDTH + HEAD_SIZE]
    cos, sin = cosine[...], sine[...]
    bias = turned_mask(starts, scalars[1], rows)
    heads = []
    for h in range(GROUP + 1):
        part = qkv[:, h * HEAD_SIZE : (h + 1) * HEAD_SIZE]
        norm = head_gains[0:1, :] if h < GROUP else head_gains[1:2, :]
        heads.append(turn(part * inv_rms(part) * norm, cos, sin).astype(BF))
        low[:, h * HEAD_SIZE : (h + 1) * HEAD_SIZE] = heads[-1]
    value = qkv[:, HEADS_WIDTH + HEAD_SIZE :].astype(BF)
    low[:, HEADS_WIDTH + HEAD_SIZE :] = value
    for h in range(GROUP):
        probs = softmax(heads[h], heads[GROUP], bias).astype(BF)
        attn[:, h * HEAD_SIZE : (h + 1) * HEAD_SIZE] = mm(probs, value).astype(BF)


def project_kernel(rows, values, weight, parts):
    split_out(mm(values[...], weight[...]), rows, parts)


def project(values, weight, rows):
    return [
        call_half(
            functools.partial(project_kernel, rows),
            which,
            [("blocks", (4, rows, weight.shape[1]), dtype)],
            [("group", values), ("whole", weight)],
        )[0]
        for which, dtype in ((0, F32), (1, BF))
    ]


def feed_kernel(rows, mid, cot, gate_up, down, normed, mixed, grad_gu, parts):
    ff = down.shape[0]
    x = group_of(mid, 0, rows)
    normed[...] = x
    both = mm(x, gate_up[...])
    gate_pre, upward = both[:, :ff], both[:, ff:]
    grad_mixed = mm_nt(group_of(cot, 0, rows), down[...])
    sigma = 1.0 / (1.0 + jnp.exp(-gate_pre))
    silu = gate_pre * sigma
    mixed[...] = (silu * upward).astype(BF)
    grad_gate = (grad_mixed * upward * sigma * (1.0 + gate_pre * (1.0 - sigma))).astype(BF)
    grad_up = (grad_mixed * silu).astype(BF)
    grad_gu[:, :ff] = grad_gate
    grad_gu[:, ff:] = grad_up
    split_out(mm_nt(grad_gu[...], gate_up[...]), rows, parts)


def attend_pull_kernel(
    rows, scalars, starts, blocks, low, raw, head_gains, cosine, sine, weight, grad_qkv, gain_out
):
    grad_attn = mm_nt(group_of(blocks, 0, rows), weight[...]).astype(BF)
    cos, sin = cosine[...], sine[...]
    bias = turned_mask(starts, scalars[1], rows)
    key = low[:, HEADS_WIDTH : HEADS_WIDTH + HEAD_SIZE]
    value = low[:, HEADS_WIDTH + HEAD_SIZE :]
    grads, grad_key, grad_value = [], 0.0, 0.0
    for h in range(GROUP):
        query = low[:, h * HEAD_SIZE : (h + 1) * HEAD_SIZE]
        probs = softmax(query, key, bias)
        grad = grad_attn[:, h * HEAD_SIZE : (h + 1) * HEAD_SIZE]
        grad_probs = mm_nt(grad, value)
        row_dot = jnp.sum(probs * grad_probs, axis=-1, keepdims=True)
        grad_scores = (probs * (grad_probs - row_dot)).astype(BF)
        grads.append(mm(grad_scores, key) * SCALE)
        grad_key = grad_key + mm_tn(grad_scores, query)
        grad_value = grad_value + mm_tn(probs.astype(BF), grad)
    grads.append(grad_key * SCALE)
    gain_sums = [0.0, 0.0]
    for h in range(GROUP + 1):
        spot = slice(h * HEAD_SIZE, (h + 1) * HEAD_SIZE)
        which = 0 if h < GROUP else 1
        back = turn(grads[h], cos, -sin)
        part = raw[:, spot]
        r = inv_rms(part)
        u = back * head_gains[which : which + 1, :]
        gain_sums[which] = gain_sums[which] + jnp.sum(back * part * r, axis=0, keepdims=True)
        pulled = r * u - part * (r * r * r) * jnp.mean(u * part, -1, keepdims=True)
        grad_qkv[:, spot] = pulled.astype(BF)
    grad_qkv[:, HEADS_WIDTH + HEAD_SIZE :] = grad_value.astype(BF)
    sums = jnp.concatenate(gain_sums, axis=1)

    @pl.when(pl.program_id(0) == 0)
    def _():
        gain_out[...] = sums

    @pl.when(pl.program_id(0) > 0)
    def _():
        gain_out[...] += sums


def project_nt_kernel(rows, grad_qkv, weight, parts):
    split_out(mm_nt(grad_qkv[...], weight[...]), rows, parts)


def weigh_kernel(orders, scalars, values, *refs):
    *grads, extra, keep, send, total = refs
    if len(grads) == 1:
        grad = grads[0][...]
    else:
        near, far = [ref[...].reshape(-1, ref.shape[2]) for ref in grads]
        grad = jnp.where(pl.program_id(0) < 2, near, far)
    term = mm_tn(values[...], grad)

    @pl.when(pl.program_id(0) == 0)
    def _():
        total[...] = term

    @pl.when(pl.program_id(0) > 0)
    def _():
        total[...] += term

    size = total.shape[0] // (2 * keep.shape[0])
    more = keep.shape[1] - size

    @pl.when(pl.program_id(0) == pl.num_programs(0) - 1)
    def _():
        for order, out in zip(orders, (keep, send)):
            for k, relative in enumerate(order):
                at = lax.bitwise_xor(scalars[0], relative) * size
                block = total[pl.ds(pl.multiple_of(at, size), size), :]
                if not more:
                    out[k] = block.astype(out.dtype)
                    continue
                line = extra[...]
                rest = total.shape[1] - line.shape[1]
                line = jnp.concatenate([line, jnp.zeros((1, rest), F32)], axis=1)
                line = jnp.broadcast_to(line, (more, total.shape[1]))
                out[k] = jnp.concatenate([block, line], axis=0).astype(out.dtype)


def weigh(values, grads, scalars, count, extra=None):
    more = 0 if extra is None else EXTRA_ROWS
    extra = jnp.zeros((1, 128), F32) if extra is None else extra
    bits = [1 << k for k in range(1, count.bit_length() - 1)]
    evens = [o for o in range(count) if not o & 1]
    evens = sorted(evens, key=lambda o: [bool(o & bit) for bit in bits])
    orders = (evens, [o ^ 1 for o in evens])
    height, width = values.shape[1], grads[0].shape[-1]
    half = (count // 2, height // count + more, width)
    if len(grads) == 1:
        grad_specs = [spec("group", grads[0].shape, 0)]
    else:
        block = (2,) + grads[0].shape[1:]
        grad_specs = [
            pl.BlockSpec(block, lambda g: (jnp.minimum(g, 1), 0, 0)),
            pl.BlockSpec(block, lambda g: (jnp.maximum(g - 2, 0), 0, 0)),
        ]
    return pl.pallas_call(
        functools.partial(weigh_kernel, orders),
        grid=(4,),
        out_shape=(jax.ShapeDtypeStruct(half, F32), jax.ShapeDtypeStruct(half, BF)),
        in_specs=[spec("scalars", (), 0), spec("group", values.shape, 0)]
        + grad_specs
        + [spec("whole", extra.shape, 0)],
        out_specs=(spec("whole", half, 0), spec("whole", half, 0)),
        scratch_shapes=[pltpu.VMEM((height, width), F32)],
        compiler_params=pltpu.CompilerParams(
            vmem_limit_bytes=24 * 2**20, dimension_semantics=("arbitrary",)
        ),
    )(scalars, values, *grads, extra)


def add_kernel(keep, got, kept, send):
    total = keep[...] + got[...].astype(F32)
    size = kept.shape[0]
    kept[...] = total[:size]
    send[...] = total[size:].astype(BF)


def halve_on(keep, got):
    bit = 2
    while keep.shape[0] > 1:
        part = (keep.shape[0] // 2,) + keep.shape[1:]
        keep, send = call(add_kernel, [(part, F32), (part, BF)], keep, got)
        got = across(send, bit)
        bit *= 2
    return keep, got


def finish_kernel(*refs):
    *terms, out, line = refs
    rows, at = out.shape[0], 0
    for keep, got in zip(terms[::2], terms[1::2]):
        total = keep[0, :rows, :] + got[0, :rows, :].astype(F32)
        out[:, at : at + total.shape[1]] = total.astype(BF)
        at += total.shape[1]
    keep, got = terms[:2]
    line[...] = (keep[0, rows : rows + 8, :] + got[0, rows : rows + 8, :].astype(F32))[:, : 2 * HEAD_SIZE]


def finish(rows, *terms):
    shape = (rows, sum(term.shape[2] for term in terms[::2]))
    outs = [(shape, BF), ((8, 2 * HEAD_SIZE), F32)]
    return call(finish_kernel, outs, *terms)


def finish_rows_kernel(*refs):
    *terms, out = refs
    at = 0
    for keep, got in zip(terms[::2], terms[1::2]):
        total = (keep[0] + got[0].astype(F32)).astype(BF)
        out[at : at + total.shape[0], :] = total
        at += total.shape[0]


def finish_rows(*terms):
    shape = (sum(term.shape[1] for term in terms[::2]), terms[0].shape[2])
    return call(finish_rows_kernel, [(shape, BF)], *terms)[0]


def local(
    tokens,
    norm_gain,
    w_query,
    w_key,
    w_value,
    w_output,
    query_gain,
    key_gain,
    mlp_gain,
    w_gate,
    w_up,
    w_down,
    lengths,
    seq_order,
    cotangent,
):
    rows, width = tokens.shape
    count = lax.axis_size("data")
    place = lax.axis_index("data")
    in_seq = lax.axis_index("seq")
    in_plane = lax.axis_index("x") * 4 + lax.axis_index("core") * 2 + in_seq
    w_rows = w_query.shape[0]
    gains = query_gain.shape[0]
    n_seq = lengths.shape[1]
    plane_rows = 8 * rows
    me = place * 8 + in_plane
    scalars = jnp.stack([place, in_seq, me]).astype(jnp.int32)

    half = HEAD_SIZE // 2
    angles = np.arange(2 * rows)[:, None] * THETA ** (-np.arange(half) * (2.0 / HEAD_SIZE))
    turns = np.stack(
        [np.tile(np.cos(angles), 2), np.concatenate([-np.sin(angles), np.sin(angles)], axis=1)]
    ).astype(np.float32)
    turns = jnp.asarray(np.stack([turns, np.roll(turns, -rows, axis=1)]))
    turns = lax.dynamic_index_in_dim(turns, in_seq, 0, False)
    cosine, sine = turns[0], turns[1]

    payload = pack(w_query, w_key, w_value, w_gate, w_up)
    marks = make_marks(
        scalars, width,
        norm_gain[None], mlp_gain[None], query_gain[None], key_gain[None], lengths, seq_order,
    )
    got = in_plane_all(payload).reshape(8 * w_rows, -1)
    marks = plane_sum(data_sum(data_sum(marks), last=True), "core")
    near = gather_chips(ordered_after(tokens, payload))
    row_weights = to_row_place(jnp.concatenate([w_output, w_down]), count)
    got, marks, near, row_weights, cot = together(got, marks, near, row_weights, cotangent)

    qkv = double([got[None, :, : 4 * HEAD_SIZE]])
    gate_up = got[None, :, 4 * HEAD_SIZE :]
    marks = plane_sum(marks, "x", "seq")
    far = flip(near, "core")
    qkv, marks, near, far, row_weights, gate_up, cot = together(
        qkv, marks, near, far, row_weights, gate_up, cot
    )

    qkv = double(qkv, last=True)
    row_weights = double([row_weights[None]])
    cot_near = gather_chips(cot)
    gain_in, gain_mid, head_gains, starts = setup(scalars, marks, n_seq)
    qkv, gain_in, near, far, row_weights, gate_up, cot_near = together(
        qkv, gain_in, near, far, row_weights, gate_up, cot_near
    )

    cot_far = flip(cot_near, "core")
    qkv_full = assemble(qkv, scalars)[0]
    kept = ()
    for which, blocks in enumerate((near, far)):
        kept = call_half(
            functools.partial(attend_kernel, rows),
            which,
            [
                ("group", (plane_rows, width), BF),
                ("group", (plane_rows, HEADS_WIDTH + HEAD_SIZE), F32),
                ("group", (plane_rows, 4 * HEAD_SIZE), BF),
                ("group", (plane_rows, HEADS_WIDTH), BF),
            ],
            [("scalars", scalars), ("group", starts), ("blocks", blocks)]
            + whole(qkv_full, gain_in, head_gains, cosine, sine),
            kept=kept,
        )
    normed_in, raw, low, attn_low = kept
    row_weights = double(row_weights, last=True)
    gate_up = double([gate_up])
    attn_low, row_weights = together(attn_low, row_weights)

    out_full, down_full = assemble(row_weights, scalars, w_output.shape[0], w_down.shape[0])
    ff = down_full.shape[0]
    part_near, part_far = project(attn_low, out_full, rows)
    sums = exchange(*merge(part_near, flip(part_far, "core")))
    gate_up = double(gate_up, last=True)
    sums, gate_up = together(sums, gate_up)

    hidden, normed_mid = call(
        hidden_kernel, [((rows, width), F32), ((rows, width), BF)], tokens, *sums, gain_mid
    )
    mid_near = gather_chips(normed_mid)
    gu_full = assemble(gate_up, scalars)[0]
    mid_near, gu_full = together(mid_near, gu_full)
    u_parts, kept = [], ()
    mid_far = flip(mid_near, "core")
    for which, mid, cot, dtype in (
        (0, mid_near, cot_near, F32),
        (1, mid_far, cot_far, BF),
    ):
        *kept, u_part = call_half(
            functools.partial(feed_kernel, rows),
            which,
            [
                ("group", (plane_rows, width), BF),
                ("group", (plane_rows, ff), BF),
                ("group", (plane_rows, 2 * ff), BF),
                ("blocks", (4, rows, width), dtype),
            ],
            [("blocks", mid), ("blocks", cot)] + whole(gu_full, down_full),
            kept=kept,
        )
        u_parts.append(u_part)
    mid_all, mixed, grad_gu = kept
    sums = exchange(*merge(u_parts[0], flip(u_parts[1], "core")))
    gu_keep, gu_send = weigh(mid_all, [grad_gu], scalars, count)
    down_keep, down_send = weigh(mixed, [cot_near, cot_far], scalars, count)
    result_near, result_far = project(mixed, down_full, rows)
    sums, result_near, result_far, gu_send, down_send = together(
        sums, result_near, result_far, gu_send, down_send
    )

    grad_hidden, grad_out = call(
        norm_pull_kernel,
        [((rows, width), F32), ((rows, width), BF)],
        hidden, cotangent, *sums, gain_mid,
    )
    out_near = gather_chips(grad_out)
    gu_got = across(gu_send, 1)
    down_got = across(down_send, 1)
    out_near, gu_keep, gu_got = together(out_near, gu_keep, gu_got)

    out_far = flip(out_near, "core")
    result_parts = merge(result_near, flip(result_far, "core"))
    gu_keep, gu_got = halve_on(gu_keep, gu_got)
    gain_parts, kept = [], ()
    for which, blocks in enumerate((out_near, out_far)):
        *kept, gain_part = call_half(
            functools.partial(attend_pull_kernel, rows),
            which,
            [
                ("group", (plane_rows, 4 * HEAD_SIZE), BF),
                ("whole", (1, 2 * HEAD_SIZE), F32),
            ],
            [("scalars", scalars), ("group", starts), ("blocks", blocks)]
            + [("group", low), ("group", raw)]
            + whole(head_gains, cosine, sine, out_full),
            kept=kept,
        )
        gain_parts.append(gain_part)
    grad_qkv = kept[0]
    gains_sum = gain_parts[0] + gain_parts[1]
    out_keep, out_send = weigh(attn_low, [out_near, out_far], scalars, count)
    out_got = across(out_send, 1)
    grad_qkv, gains_sum, result_parts, gu_keep, gu_got, down_keep, down_got, out_keep, out_got = together(
        grad_qkv, gains_sum, result_parts, gu_keep, gu_got, down_keep, down_got, out_keep, out_got
    )

    qkv_keep, qkv_send = weigh(normed_in, [grad_qkv], scalars, count, gains_sum)
    qkv_got = across(qkv_send, 1)
    part_near, part_far = [
        call_half(
            functools.partial(project_nt_kernel, rows),
            which,
            [("blocks", (4, rows, width), dtype)],
            [("group", grad_qkv)] + whole(qkv_full),
        )[0]
        for which, dtype in ((0, F32), (1, BF))
    ]
    sums = exchange(*merge(part_near, flip(part_far, "core")))
    down_keep, down_got = halve_on(down_keep, down_got)
    qkv_keep, qkv_got, out_keep, out_got, result_parts = together(
        qkv_keep, qkv_got, out_keep, out_got, result_parts
    )

    qkv_keep, qkv_got = halve_on(qkv_keep, qkv_got)
    out_keep, out_got = halve_on(out_keep, out_got)
    grad_tokens = call(
        norm_pull_kernel, [((rows, width), F32)], tokens, grad_hidden, *sums, gain_in
    )[0]
    result_sums = exchange(*result_parts)
    qkv_keep, qkv_got, out_keep, out_got, down_keep, down_got, grad_tokens = together(
        qkv_keep, qkv_got, out_keep, out_got, down_keep, down_got, grad_tokens
    )

    got, gains_sum = finish(8 * w_rows, qkv_keep, qkv_got, gu_keep, gu_got)
    got = in_plane_all(got.reshape(8, w_rows, got.shape[1]))
    row_grads = to_row_owner(finish_rows(out_keep, out_got, down_keep, down_got), count)
    gains_sum = plane_sum(gains_sum)
    result = call(result_kernel, [((rows, width), BF)], hidden, *result_sums)[0]
    me = me * gains
    grad_query_gain = lax.dynamic_slice_in_dim(gains_sum[0, :HEAD_SIZE], me, gains)
    grad_key_gain = lax.dynamic_slice_in_dim(gains_sum[0, HEAD_SIZE:], me, gains)
    row_grads = row_grads.astype(F32)
    (grad_w_query, grad_w_key, grad_w_value), grad_norm_gain = unpack(
        got, 0, norm_gain, w_query, w_key, w_value
    )
    (grad_w_gate, grad_w_up), grad_mlp_gain = unpack(got, 4 * HEAD_SIZE, mlp_gain, w_gate, w_up)
    out_rows = w_output.shape[0]
    return (
        result,
        grad_tokens,
        grad_norm_gain,
        grad_w_query,
        grad_w_key,
        grad_w_value,
        row_grads[:out_rows],
        grad_query_gain,
        grad_key_gain,
        grad_mlp_gain,
        grad_w_gate,
        grad_w_up,
        row_grads[out_rows:],
    )


def solution(mesh):
    fsdp, seq = mesh.shape["fsdp"], mesh.shape["seq"]
    fine = Mesh(np.asarray(mesh.devices).reshape(fsdp // 4, 2, 2, seq), ALL)
    matrix, vector, group = P(ALL, None), P(ALL), P(ALL[:3], None)
    placed = (
        matrix, vector, matrix, matrix, matrix, matrix, vector, vector, vector,
        matrix, matrix, matrix, group, group, matrix,
    )
    outs = (
        matrix, matrix, vector, matrix, matrix, matrix, matrix, vector, vector, vector,
        matrix, matrix, matrix,
    )
    return jax.shard_map(local, mesh=fine, in_specs=placed, out_specs=outs, check_vma=False)
```

```python
import functools

import jax
import jax.numpy as jnp
import numpy as np
from jax import lax
from jax.experimental import pallas as pl
from jax.experimental.pallas import tpu as pltpu
from jax.sharding import Mesh, PartitionSpec as P

QUERY_HEADS = 16
KEY_VALUE_HEADS = 8
HEAD_SIZE = 128
GROUP = QUERY_HEADS // KEY_VALUE_HEADS
HEADS_WIDTH = GROUP * HEAD_SIZE

EPS = 1e-06
THETA = 1000000.0
SCALE = HEAD_SIZE ** (-0.5)
EXTRA_ROWS = 16

ALL = ("data", "x", "core", "seq")
BF = jnp.bfloat16
F32 = jnp.float32
SWAP = [(0, 1), (1, 0)]


def mm(a, b):
    return lax.dot_general(a, b, (((1,), (0,)), ((), ())), preferred_element_type=F32)


def mm_nt(a, b):
    return lax.dot_general(a, b, (((1,), (1,)), ((), ())), preferred_element_type=F32)


def mm_tn(a, b):
    return lax.dot_general(a, b, (((0,), (0,)), ((), ())), preferred_element_type=F32)


def together(*values):
    return lax.optimization_barrier(values)


def flip(value, axis):
    return lax.ppermute(value, axis, SWAP)


def flip_diagonal(value):
    return lax.ppermute(value, ("x", "seq"), [(i, i ^ 3) for i in range(4)])


def gather_chips(block):
    from_d = flip_diagonal(block)
    return jnp.stack([block, flip(block, "seq"), flip(block, "x"), from_d])


def exchange(own, to_y, to_x, to_d):
    from_d = flip_diagonal(to_d)
    return own, flip(to_y, "seq"), flip(to_x, "x"), from_d


def in_plane_all(payload):
    return lax.all_to_all(payload, ALL[1:], split_axis=0, concat_axis=0, tiled=True)


def to_row_place(block, count):
    route = [(count * j + d, d * 8 + j) for d in range(count) for j in range(8)]
    return lax.ppermute(block, ALL, route)


def doubling_orders(count):
    orders, bit = [[0]], count // 2
    while bit:
        orders.append([o ^ bit for order in orders for o in order])
        bit //= 2
    return orders


def across(value, bit):
    return lax.ppermute(value, "data", [(d, d ^ bit) for d in range(lax.axis_size("data"))])


def double(arrays, last=False):
    arrays, bit = list(arrays), lax.axis_size("data") // 2
    while bit > 1 and not last:
        arrays.append(across(jnp.concatenate(arrays), bit))
        bit //= 2
    if last:
        arrays.append(across(jnp.concatenate(arrays), 1))
    return arrays


def plane_sum(value, *axes):
    for axis in axes or ("core", "x", "seq"):
        value = value + flip(value, axis)
    return value


def data_sum(value, last=False):
    bit = lax.axis_size("data") // 2
    while bit > 1 and not last:
        value = value + across(value, bit)
        bit //= 2
    return value + across(value, 1) if last else value


def to_row_owner(block, count):
    route = [(d * 8 + j, count * j + d) for d in range(count) for j in range(8)]
    return lax.ppermute(block, ALL, route)


def spec(kind, shape, at):
    zeros = (0,) * (len(shape) - 1)
    if kind == "blocks":
        return pl.BlockSpec((2,) + shape[1:], lambda g: (g,) + zeros)
    if kind == "half":
        return pl.BlockSpec((shape[0] // 2,) + shape[1:], lambda g: (g,) + zeros)
    if kind == "group":
        return pl.BlockSpec((shape[0] // 4,) + shape[1:], lambda g: (at + g,) + zeros)
    if kind == "scalars":
        return pl.BlockSpec(memory_space=pltpu.SMEM)
    if kind == "kept":
        return pl.BlockSpec(memory_space=pl.ANY)
    return pl.BlockSpec(shape, lambda g: (0,) + zeros)


def call_half(kernel, which, outs, args, kept=(), scratch=()):
    at = 2 * which
    given = list(args) + [("kept", array) for array in kept]
    aliases = {len(args) + k: k for k in range(len(kept))}
    n_args = len(args)

    def body(*refs):
        kernel(*refs[:n_args], *refs[n_args + len(kept) :])

    return pl.pallas_call(
        body,
        grid=(2,),
        out_shape=tuple(jax.ShapeDtypeStruct(shape, dtype) for _, shape, dtype in outs),
        in_specs=[spec(kind, arg.shape, at) for kind, arg in given],
        out_specs=tuple(spec(kind, shape, at) for kind, shape, _ in outs),
        scratch_shapes=list(scratch),
        input_output_aliases=aliases,
        compiler_params=pltpu.CompilerParams(
            vmem_limit_bytes=24 * 2**20, dimension_semantics=("arbitrary",)
        ),
    )(*[arg for _, arg in given])


def call(kernel, outs, *args):
    vmem = pl.BlockSpec(memory_space=pltpu.VMEM)
    return pl.pallas_call(
        kernel,
        out_shape=tuple(jax.ShapeDtypeStruct(shape, dtype) for shape, dtype in outs),
        in_specs=[vmem for _ in args],
        out_specs=tuple(vmem for _ in outs),
        compiler_params=pltpu.CompilerParams(vmem_limit_bytes=12 * 2**20),
    )(*args)


def whole(*arrays):
    return [("whole", array) for array in arrays]


def pack_kernel(widths, *refs):
    *weights, out = refs
    for j in range(8):
        at = 0
        for width, ref in zip(widths, weights):
            out[j, :, at : at + width] = ref[:, j * width : (j + 1) * width]
            at += width


def pack(*weights):
    widths = [w.shape[1] // 8 for w in weights]
    shape = (8, weights[0].shape[0], sum(widths))
    return pl.pallas_call(
        functools.partial(pack_kernel, widths),
        grid=(1,),
        out_shape=jax.ShapeDtypeStruct(shape, BF),
        in_specs=[spec("whole", w.shape, 0) for w in weights],
        out_specs=spec("whole", shape, 0),
    )(*weights)


def marks_kernel(scalars, norm_gain, mlp_gain, query_gain, key_gain, lengths, seq_order, out):
    width = out.shape[1]

    def placed(ref, at):
        line = ref[...].astype(F32)
        line = jnp.concatenate([line, jnp.zeros((1, width - line.shape[1]), F32)], axis=1)
        return pltpu.roll(line, at * ref.shape[1], 1)

    lines = [placed(ref, scalars[2]) for ref in (norm_gain, mlp_gain, query_gain, key_gain)]
    once = (1 - scalars[1]).astype(F32)
    lines += [placed(ref, scalars[2] // 2) * once for ref in (lengths, seq_order)]
    lines.append(jnp.zeros((2, width), F32))
    out[...] = jnp.concatenate(lines, axis=0).astype(BF)


def make_marks(scalars, width, *values):
    vmem = pl.BlockSpec(memory_space=pltpu.VMEM)
    return pl.pallas_call(
        marks_kernel,
        out_shape=jax.ShapeDtypeStruct((8, width), BF),
        in_specs=[pl.BlockSpec(memory_space=pltpu.SMEM)] + [vmem for _ in values],
        out_specs=vmem,
    )(scalars, *values)


def setup_kernel(n_seq, scalars, marks, gain_in, gain_mid, head_gains, starts):
    rows = marks[...].astype(F32)
    gain_in[...] = rows[0:1]
    gain_mid[...] = rows[1:2]
    head_gains[...] = rows[2:4, :HEAD_SIZE]
    width = rows.shape[1]
    lane = lax.broadcasted_iota(jnp.int32, (1, 128), 1).astype(F32)
    for k, relative in enumerate((0, 2, 1, 3)):
        back = width - lax.bitwise_xor(scalars[2] // 2, relative) * n_seq
        lengths, order = [pltpu.roll(rows[q : q + 1], back, 1)[:, :128] for q in (4, 5)]
        at = jnp.zeros((1, 1), F32)
        for q in range(n_seq):
            starts[k, q : q + 1, :] = jnp.broadcast_to(at, (1, 128))
            mine = (lane == order[:, q : q + 1]) & (lane < n_seq)
            at = at + jnp.sum(jnp.where(mine, lengths, 0.0), axis=1, keepdims=True)
        starts[k, n_seq:, :] = jnp.full((8 - n_seq, 128), 1e9, F32)


def setup(scalars, marks, n_seq):
    width = marks.shape[1]
    outs = [((1, width), F32), ((1, width), F32), ((2, HEAD_SIZE), F32), ((4, 8, 128), F32)]
    vmem = pl.BlockSpec(memory_space=pltpu.VMEM)
    return pl.pallas_call(
        functools.partial(setup_kernel, n_seq),
        out_shape=tuple(jax.ShapeDtypeStruct(shape, dtype) for shape, dtype in outs),
        in_specs=[pl.BlockSpec(memory_space=pltpu.SMEM), vmem],
        out_specs=tuple(vmem for _ in outs),
    )(scalars, marks)


def assemble_kernel(orders, cuts, scalars, *refs):
    arrays, outs = refs[: len(orders)], refs[len(orders) :]
    for order, ref in zip(orders, arrays):
        for k, relative in enumerate(order):
            place, start = lax.bitwise_xor(scalars[0], relative), 0
            for size, out in zip(cuts, outs):
                at = pl.multiple_of(place * size, size)
                out[pl.ds(at, size), :] = ref[k, start : start + size, :]
                start += size


def assemble(arrays, scalars, *cuts):
    count = sum(array.shape[0] for array in arrays)
    orders = doubling_orders(count)
    _, size, width = arrays[0].shape
    cuts = cuts or (size,)
    if any(cut % 16 for cut in cuts):
        came = jnp.concatenate(arrays)
        at = jnp.asarray(np.argsort([o for order in orders for o in order]))
        came = came[at[jnp.arange(count) ^ scalars[0]]]
        ends = np.cumsum(cuts)
        return [came[:, b - a : b].reshape(count * a, width) for a, b in zip(cuts, ends)]
    vmem = pl.BlockSpec(memory_space=pltpu.VMEM)
    return pl.pallas_call(
        functools.partial(assemble_kernel, orders, cuts),
        out_shape=tuple(jax.ShapeDtypeStruct((count * cut, width), BF) for cut in cuts),
        in_specs=[pl.BlockSpec(memory_space=pltpu.SMEM)] + [vmem for _ in arrays],
        out_specs=tuple(vmem for _ in cuts),
    )(scalars, *arrays)


def unpack_kernel(widths, start, scalars, got, gain, *refs):
    weights, outs = refs[: len(widths)], refs[len(widths) : -2]
    gain_out, head_gains = refs[-2:]
    rows, sums, line = gain.shape[0], 0.0, 0.0
    for j in range(8):
        at = start
        for width, weight, out in zip(widths, weights, outs):
            piece = got[j, :rows, at : at + width].astype(F32)
            out[:, j * width : (j + 1) * width] = piece
            kept = weight[:, j * width : (j + 1) * width].astype(F32)
            sums = sums + jnp.sum(piece * kept, axis=1, keepdims=True)
            at += width
        line = line + got[j, rows : rows + 8, : 2 * HEAD_SIZE].astype(F32)
    gain_out[...] = sums / gain[...]
    each = head_gains.shape[1]
    for k in range(2):
        part = line[0:1, k * HEAD_SIZE : (k + 1) * HEAD_SIZE]
        back = lax.rem(HEAD_SIZE - scalars[2] * each, HEAD_SIZE)
        head_gains[k : k + 1, :] = pltpu.roll(part, back, 1)[:, :each]


def unpack(got, start, gain, scalars, gains, *weights):
    widths = [w.shape[1] // 8 for w in weights]
    outs = [(w.shape, F32) for w in weights] + [((gain.shape[0], 1), F32), ((2, gains), F32)]
    vmem = pl.BlockSpec(memory_space=pltpu.VMEM)
    *grads, gain_grad, head_gains = pl.pallas_call(
        functools.partial(unpack_kernel, widths, start),
        out_shape=tuple(jax.ShapeDtypeStruct(shape, dtype) for shape, dtype in outs),
        in_specs=[pl.BlockSpec(memory_space=pltpu.SMEM)] + [vmem] * (2 + len(weights)),
        out_specs=tuple(vmem for _ in outs),
        compiler_params=pltpu.CompilerParams(vmem_limit_bytes=12 * 2**20),
    )(scalars, got, gain.astype(F32)[:, None], *weights)
    return grads, gain_grad[:, 0], head_gains


def merge_kernel(near, other, own, to_y, to_x, to_d):
    own[...] = near[0] + other[0].astype(F32)
    for k, out in ((1, to_y), (2, to_x), (3, to_d)):
        out[...] = (near[k] + other[k].astype(F32)).astype(BF)


def merge_all_kernel(scalars, near, other, own, out):
    own[...] = near[0] + other[0].astype(F32)
    for k in range(4):
        part = near[k] + other[k].astype(F32) if k else jnp.zeros_like(near[0])
        out[lax.bitwise_xor(scalars[3], k)] = part.astype(BF)


def merge_all(scalars, near, other):
    vmem = pl.BlockSpec(memory_space=pltpu.VMEM)
    return pl.pallas_call(
        merge_all_kernel,
        out_shape=(
            jax.ShapeDtypeStruct(near.shape[1:], F32),
            jax.ShapeDtypeStruct(near.shape, BF),
        ),
        in_specs=[pl.BlockSpec(memory_space=pltpu.SMEM), vmem, vmem],
        out_specs=(vmem, vmem),
        compiler_params=pltpu.CompilerParams(vmem_limit_bytes=12 * 2**20),
    )(scalars, near, other)


def merge(near, other):
    shape = near.shape[1:]
    return call(merge_kernel, [(shape, F32)] + [(shape, BF)] * 3, near, other)


def inv_rms(values):
    return lax.rsqrt(jnp.mean(values * values, axis=-1, keepdims=True) + EPS)


def summed(own, from_y, from_x, from_d, rows):
    total = own[:rows]
    for ref in (from_y, from_x, from_d):
        total = total + ref[:rows].astype(F32)
    return total


def hidden_kernel(tokens, own, from_y, from_x, from_d, gain, hidden, normed):
    total = tokens[...].astype(F32) + summed(own, from_y, from_x, from_d, tokens.shape[0])
    hidden[...] = total
    normed[...] = (total * inv_rms(total) * gain[...]).astype(BF)


def result_kernel(hidden, own, others, result):
    total = hidden[...] + own[...]
    for k in range(4):
        total = total + others[k].astype(F32)
    result[...] = total.astype(BF)


def norm_pull_kernel(values, base, own, from_y, from_x, from_d, gain, out, *low):
    v = values[...].astype(F32)
    u = summed(own, from_y, from_x, from_d, v.shape[0]) * gain[...]
    r = inv_rms(v)
    total = base[...].astype(F32) + r * u - v * (r * r * r) * jnp.mean(u * v, -1, keepdims=True)
    out[...] = total
    for ref in low:
        ref[...] = total.astype(BF)


def turn(values, cosine, sine):
    return values * cosine + pltpu.roll(values, HEAD_SIZE // 2, 1) * sine


def turned_mask(starts, in_seq, rows):
    span = 2 * rows

    def ids(dim):
        shape = (span, 1) if dim == 0 else (1, span)
        at = lax.broadcasted_iota(jnp.int32, shape, dim)
        return lax.rem(at + in_seq * rows, span).astype(F32)

    def of_sequence(row_ids):
        return sum((row_ids >= starts[0, k : k + 1, 0:1]).astype(F32) for k in range(8))

    down, along = ids(0), ids(1)
    allowed = (along <= down) & (of_sequence(along) == of_sequence(down))
    return jnp.where(allowed, 0.0, -1e30).astype(F32)


def softmax(query, key, bias):
    scores = mm_nt(query, key) * SCALE + bias
    exp_scores = jnp.exp(scores - jnp.max(scores, axis=-1, keepdims=True))
    return exp_scores / jnp.sum(exp_scores, axis=-1, keepdims=True)


def group_of(blocks, start, rows):
    return jnp.concatenate([blocks[0, start : start + rows, :], blocks[1, start : start + rows, :]])


def split_out(product, rows, parts):
    for k in range(2):
        parts[k, :rows, :] = product[k * rows : (k + 1) * rows].astype(parts.dtype)


def attend_kernel(
    rows, scalars, starts, blocks, weight, gain, head_gains, cosine, sine, *outs
):
    normed, raw, low, attn = outs
    x = group_of(blocks, 0, rows).astype(F32)
    x = (x * inv_rms(x) * gain[...]).astype(BF)
    normed[...] = x
    qkv = mm(x, weight[...])
    raw[...] = qkv[:, : HEADS_WIDTH + HEAD_SIZE]
    cos, sin = cosine[...], sine[...]
    bias = turned_mask(starts, scalars[1], rows)
    heads = []
    for h in range(GROUP + 1):
        part = qkv[:, h * HEAD_SIZE : (h + 1) * HEAD_SIZE]
        norm = head_gains[0:1, :] if h < GROUP else head_gains[1:2, :]
        heads.append(turn(part * inv_rms(part) * norm, cos, sin).astype(BF))
        low[:, h * HEAD_SIZE : (h + 1) * HEAD_SIZE] = heads[-1]
    value = qkv[:, HEADS_WIDTH + HEAD_SIZE :].astype(BF)
    low[:, HEADS_WIDTH + HEAD_SIZE :] = value
    for h in range(GROUP):
        probs = softmax(heads[h], heads[GROUP], bias).astype(BF)
        attn[:, h * HEAD_SIZE : (h + 1) * HEAD_SIZE] = mm(probs, value).astype(BF)


def project_kernel(rows, values, weight, parts):
    split_out(mm(values[...], weight[...]), rows, parts)


def project(values, weight, rows):
    return [
        call_half(
            functools.partial(project_kernel, rows),
            which,
            [("blocks", (4, rows, weight.shape[1]), dtype)],
            [("group", values), ("whole", weight)],
        )[0]
        for which, dtype in ((0, F32), (1, BF))
    ]


def feed_kernel(rows, mid, cot, w_gate, w_up, down, normed, mixed, grad_gu, parts):
    ff = down.shape[0]
    x = group_of(mid, 0, rows)
    normed[...] = x
    gate_pre = mm(x, w_gate[...])
    upward = mm(x, w_up[...])
    grad_mixed = mm_nt(group_of(cot, 0, rows), down[...])
    sigma = 1.0 / (1.0 + jnp.exp(-gate_pre))
    silu = gate_pre * sigma
    mixed[...] = (silu * upward).astype(BF)
    grad_gate = (grad_mixed * upward * sigma * (1.0 + gate_pre * (1.0 - sigma))).astype(BF)
    grad_up = (grad_mixed * silu).astype(BF)
    grad_gu[:, :ff] = grad_gate
    grad_gu[:, ff:] = grad_up
    split_out(mm_nt(grad_gate, w_gate[...]) + mm_nt(grad_up, w_up[...]), rows, parts)


def attend_pull_kernel(
    rows, scalars, starts, blocks, low, raw, head_gains, cosine, sine, weight, grad_qkv, gain_out
):
    grad_attn = mm_nt(group_of(blocks, 0, rows), weight[...]).astype(BF)
    cos, sin = cosine[...], sine[...]
    bias = turned_mask(starts, scalars[1], rows)
    key = low[:, HEADS_WIDTH : HEADS_WIDTH + HEAD_SIZE]
    value = low[:, HEADS_WIDTH + HEAD_SIZE :]
    grads, grad_key, grad_value = [], 0.0, 0.0
    for h in range(GROUP):
        query = low[:, h * HEAD_SIZE : (h + 1) * HEAD_SIZE]
        probs = softmax(query, key, bias)
        grad = grad_attn[:, h * HEAD_SIZE : (h + 1) * HEAD_SIZE]
        grad_probs = mm_nt(grad, value)
        row_dot = jnp.sum(probs * grad_probs, axis=-1, keepdims=True)
        grad_scores = (probs * (grad_probs - row_dot)).astype(BF)
        grads.append(mm(grad_scores, key) * SCALE)
        grad_key = grad_key + mm_tn(grad_scores, query)
        grad_value = grad_value + mm_tn(probs.astype(BF), grad)
    grads.append(grad_key * SCALE)
    gain_sums = [0.0, 0.0]
    for h in range(GROUP + 1):
        spot = slice(h * HEAD_SIZE, (h + 1) * HEAD_SIZE)
        which = 0 if h < GROUP else 1
        back = turn(grads[h], cos, -sin)
        part = raw[:, spot]
        r = inv_rms(part)
        u = back * head_gains[which : which + 1, :]
        gain_sums[which] = gain_sums[which] + jnp.sum(back * part * r, axis=0, keepdims=True)
        pulled = r * u - part * (r * r * r) * jnp.mean(u * part, -1, keepdims=True)
        grad_qkv[:, spot] = pulled.astype(BF)
    grad_qkv[:, HEADS_WIDTH + HEAD_SIZE :] = grad_value.astype(BF)
    sums = jnp.concatenate(gain_sums, axis=1)

    @pl.when(pl.program_id(0) == 0)
    def _():
        gain_out[...] = sums

    @pl.when(pl.program_id(0) > 0)
    def _():
        gain_out[...] += sums


def project_nt_kernel(rows, grad_qkv, weight, parts):
    split_out(mm_nt(grad_qkv[...], weight[...]), rows, parts)


def weigh_kernel(orders, scalars, values, *refs):
    *grads, extra, keep, send, total = refs
    if len(grads) == 1:
        grad = grads[0][...]
    else:
        near, far = [ref[...].reshape(-1, ref.shape[2]) for ref in grads]
        grad = jnp.where(pl.program_id(0) < 2, near, far)
    term = mm_tn(values[...], grad)

    @pl.when(pl.program_id(0) == 0)
    def _():
        total[...] = term

    @pl.when(pl.program_id(0) > 0)
    def _():
        total[...] += term

    size = total.shape[0] // (2 * keep.shape[0])
    more = keep.shape[1] - size

    @pl.when(pl.program_id(0) == pl.num_programs(0) - 1)
    def _():
        for order, out in zip(orders, (keep, send)):
            for k, relative in enumerate(order):
                at = lax.bitwise_xor(scalars[0], relative) * size
                block = total[pl.ds(pl.multiple_of(at, size), size), :]
                if not more:
                    out[k] = block.astype(out.dtype)
                    continue
                line = extra[...]
                rest = total.shape[1] - line.shape[1]
                line = jnp.concatenate([line, jnp.zeros((1, rest), F32)], axis=1)
                line = jnp.broadcast_to(line, (more, total.shape[1]))
                out[k] = jnp.concatenate([block, line], axis=0).astype(out.dtype)


def weigh(values, grads, scalars, count, extra=None):
    more = 0 if extra is None else EXTRA_ROWS
    extra = jnp.zeros((1, 128), F32) if extra is None else extra
    bits = [1 << k for k in range(1, count.bit_length() - 1)]
    evens = [o for o in range(count) if not o & 1]
    evens = sorted(evens, key=lambda o: [bool(o & bit) for bit in bits])
    orders = (evens, [o ^ 1 for o in evens])
    height, width = values.shape[1], grads[0].shape[-1]
    half = (count // 2, height // count + more, width)
    if len(grads) == 1:
        grad_specs = [spec("group", grads[0].shape, 0)]
    else:
        block = (2,) + grads[0].shape[1:]
        grad_specs = [
            pl.BlockSpec(block, lambda g: (jnp.minimum(g, 1), 0, 0)),
            pl.BlockSpec(block, lambda g: (jnp.maximum(g - 2, 0), 0, 0)),
        ]
    return pl.pallas_call(
        functools.partial(weigh_kernel, orders),
        grid=(4,),
        out_shape=(jax.ShapeDtypeStruct(half, F32), jax.ShapeDtypeStruct(half, BF)),
        in_specs=[spec("scalars", (), 0), spec("group", values.shape, 0)]
        + grad_specs
        + [spec("whole", extra.shape, 0)],
        out_specs=(spec("whole", half, 0), spec("whole", half, 0)),
        scratch_shapes=[pltpu.VMEM((height, width), F32)],
        compiler_params=pltpu.CompilerParams(
            vmem_limit_bytes=24 * 2**20, dimension_semantics=("arbitrary",)
        ),
    )(scalars, values, *grads, extra)


def add_kernel(keep, got, kept, send):
    total = keep[...] + got[...].astype(F32)
    size = kept.shape[0]
    kept[...] = total[:size]
    send[...] = total[size:].astype(BF)


def halve_add(keep, got):
    part = (keep.shape[0] // 2,) + keep.shape[1:]
    return call(add_kernel, [(part, F32), (part, BF)], keep, got)


def halve_on(keep, send):
    got, bit = across(send, 2), 4
    while keep.shape[0] > 1:
        keep, send = halve_add(keep, got)
        got = across(send, bit)
        bit *= 2
    return keep, got


def finish_kernel(rows, *refs):
    *terms, out = refs
    at = 0
    for keep, got in zip(terms[::2], terms[1::2]):
        size = 8 * rows
        total = (keep[0, :size, :] + got[0, :size, :].astype(F32)).astype(BF)
        width = total.shape[1]
        for j in range(8):
            out[j, :rows, at : at + width] = total[j * rows : (j + 1) * rows]
            if at == 0:
                line = keep[0, size : size + 8, :] + got[0, size : size + 8, :].astype(F32)
                out[j, rows:, :width] = line.astype(BF)
            else:
                out[j, rows:, at : at + width] = jnp.zeros((8, width), BF)
        at += width


def finish(rows, *terms):
    shape = (8, rows + 8, sum(term.shape[2] for term in terms[::2]))
    return call(functools.partial(finish_kernel, rows), [(shape, BF)], *terms)[0]


def finish_rows_kernel(*refs):
    *terms, out = refs
    at = 0
    for keep, got in zip(terms[::2], terms[1::2]):
        total = (keep[0] + got[0].astype(F32)).astype(BF)
        out[at : at + total.shape[0], :] = total
        at += total.shape[0]


def finish_rows(*terms):
    shape = (sum(term.shape[1] for term in terms[::2]), terms[0].shape[2])
    return call(finish_rows_kernel, [(shape, BF)], *terms)[0]


def local(
    tokens,
    norm_gain,
    w_query,
    w_key,
    w_value,
    w_output,
    query_gain,
    key_gain,
    mlp_gain,
    w_gate,
    w_up,
    w_down,
    lengths,
    seq_order,
    cotangent,
):
    rows, width = tokens.shape
    count = lax.axis_size("data")
    place = lax.axis_index("data")
    in_seq = lax.axis_index("seq")
    in_plane = lax.axis_index("x") * 4 + lax.axis_index("core") * 2 + in_seq
    w_rows = w_query.shape[0]
    gains = query_gain.shape[0]
    n_seq = lengths.shape[1]
    plane_rows = 8 * rows
    me = place * 8 + in_plane
    in_chips = lax.axis_index("x") * 2 + in_seq
    scalars = jnp.stack([place, in_seq, me, in_chips]).astype(jnp.int32)

    half = HEAD_SIZE // 2
    angles = np.arange(2 * rows)[:, None] * THETA ** (-np.arange(half) * (2.0 / HEAD_SIZE))
    turns = np.stack(
        [np.tile(np.cos(angles), 2), np.concatenate([-np.sin(angles), np.sin(angles)], axis=1)]
    ).astype(np.float32)
    turns = jnp.asarray(np.stack([turns, np.roll(turns, -rows, axis=1)]))
    turns = lax.dynamic_index_in_dim(turns, in_seq, 0, False)
    cosine, sine = turns[0], turns[1]

    payload = pack(w_query, w_key, w_value)
    marks = make_marks(
        scalars, width,
        norm_gain[None], mlp_gain[None], query_gain[None], key_gain[None], lengths, seq_order,
    )
    got = in_plane_all(payload).reshape(8 * w_rows, -1)
    marks = data_sum(data_sum(marks), last=True)
    near = gather_chips(tokens)
    payload, row_weights = together(payload, jnp.concatenate([w_output, w_down]))
    row_weights = to_row_place(row_weights, count)
    got, marks, near, row_weights, cot, gate, up = together(
        got, marks, near, row_weights, cotangent, w_gate, w_up
    )

    qkv = double([got[None]])
    marks = plane_sum(marks)
    far = flip(near, "core")
    gate = in_plane_all(pack(gate)).reshape(1, 8 * w_rows, -1)
    qkv, marks, near, far, row_weights, gate, up, cot = together(
        qkv, marks, near, far, row_weights, gate, up, cot
    )

    qkv = double(qkv, last=True)
    row_weights = double([row_weights[None]])
    cot_near = gather_chips(cot)
    gain_in, gain_mid, head_gains, starts = setup(scalars, marks, n_seq)
    up = in_plane_all(pack(up)).reshape(1, 8 * w_rows, -1)
    qkv, gain_in, near, far, row_weights, gate, up, cot_near = together(
        qkv, gain_in, near, far, row_weights, gate, up, cot_near
    )

    cot_far = flip(cot_near, "core")
    qkv_full = assemble(qkv, scalars)[0]
    kept = ()
    for which, blocks in enumerate((near, far)):
        kept = call_half(
            functools.partial(attend_kernel, rows),
            which,
            [
                ("group", (plane_rows, width), BF),
                ("group", (plane_rows, HEADS_WIDTH + HEAD_SIZE), F32),
                ("group", (plane_rows, 4 * HEAD_SIZE), BF),
                ("group", (plane_rows, HEADS_WIDTH), BF),
            ],
            [("scalars", scalars), ("group", starts), ("blocks", blocks)]
            + whole(qkv_full, gain_in, head_gains, cosine, sine),
            kept=kept,
        )
    normed_in, raw, low, attn_low = kept
    row_weights = double(row_weights, last=True)
    gate = double([gate])
    attn_low, row_weights, gate, up = together(attn_low, row_weights, gate, up)

    out_full, down_full = assemble(row_weights, scalars, w_output.shape[0], w_down.shape[0])
    ff = down_full.shape[0]
    part_near, part_far = project(attn_low, out_full, rows)
    sums = exchange(*merge(part_near, flip(part_far, "core")))
    gate = double(gate, last=True)
    up = double([up])
    sums, gate, up = together(sums, gate, up)

    hidden, normed_mid = call(
        hidden_kernel, [((rows, width), F32), ((rows, width), BF)], tokens, *sums, gain_mid
    )
    mid_near = gather_chips(normed_mid)
    gate_full = assemble(gate, scalars)[0]
    up_full = assemble(double(up, last=True), scalars)[0]
    mid_near, gate_full, up_full = together(mid_near, gate_full, up_full)
    u_parts, kept = [], ()
    mid_far = flip(mid_near, "core")
    for which, mid, cot, dtype in (
        (0, mid_near, cot_near, F32),
        (1, mid_far, cot_far, BF),
    ):
        *kept, u_part = call_half(
            functools.partial(feed_kernel, rows),
            which,
            [
                ("group", (plane_rows, width), BF),
                ("group", (plane_rows, ff), BF),
                ("group", (plane_rows, 2 * ff), BF),
                ("blocks", (4, rows, width), dtype),
            ],
            [("blocks", mid), ("blocks", cot)] + whole(gate_full, up_full, down_full),
            kept=kept,
        )
        u_parts.append(u_part)
    mid_all, mixed, grad_gu = kept
    sums = exchange(*merge(u_parts[0], flip(u_parts[1], "core")))
    down_keep, down_send = weigh(mixed, [cot_near, cot_far], scalars, count)
    down_got = across(down_send, 1)
    mid_all, _ = together(mid_all, down_send)
    gu_keep, gu_send = weigh(mid_all, [grad_gu], scalars, count)
    result_near, result_far = project(mixed, down_full, rows)
    result_own, result_parts = merge_all(scalars, result_near, flip(result_far, "core"))
    sums, result_own, result_parts, gu_send, down_got = together(
        sums, result_own, result_parts, gu_send, down_got
    )

    grad_hidden, grad_out = call(
        norm_pull_kernel,
        [((rows, width), F32), ((rows, width), BF)],
        hidden, cotangent, *sums, gain_mid,
    )
    out_near = gather_chips(grad_out)
    gu_got = across(gu_send, 1)
    down_keep, down_got = halve_on(*halve_add(down_keep, down_got))
    gu_keep, gu_send = halve_add(gu_keep, gu_got)
    out_near, gu_keep, gu_send, down_keep, down_got = together(
        out_near, gu_keep, gu_send, down_keep, down_got
    )

    out_far = flip(out_near, "core")
    gu_keep, gu_got = halve_on(gu_keep, gu_send)
    down_rows = to_row_owner(finish_rows(down_keep, down_got), count)
    gain_parts, kept = [], ()
    for which, blocks in enumerate((out_near, out_far)):
        *kept, gain_part = call_half(
            functools.partial(attend_pull_kernel, rows),
            which,
            [
                ("group", (plane_rows, 4 * HEAD_SIZE), BF),
                ("whole", (1, 2 * HEAD_SIZE), F32),
            ],
            [("scalars", scalars), ("group", starts), ("blocks", blocks)]
            + [("group", low), ("group", raw)]
            + whole(head_gains, cosine, sine, out_full),
            kept=kept,
        )
        gain_parts.append(gain_part)
    grad_qkv = kept[0]
    gains_sum = gain_parts[0] + gain_parts[1]
    qkv_keep, qkv_send = weigh(normed_in, [grad_qkv], scalars, count, gains_sum)
    part_near, part_far = [
        call_half(
            functools.partial(project_nt_kernel, rows),
            which,
            [("blocks", (4, rows, width), dtype)],
            [("group", grad_qkv)] + whole(qkv_full),
        )[0]
        for which, dtype in ((0, F32), (1, BF))
    ]
    part_near, part_far, qkv_keep, qkv_send, attn_low, down_rows, gu_keep, gu_got = together(
        part_near, part_far, qkv_keep, qkv_send, attn_low, down_rows, gu_keep, gu_got
    )

    qkv_got = across(qkv_send, 1)
    sums = exchange(*merge(part_near, flip(part_far, "core")))
    out_keep, out_send = weigh(attn_low, [out_near, out_far], scalars, count)
    out_got = across(out_send, 1)
    result_got = lax.all_to_all(
        result_parts, ("x", "seq"), split_axis=0, concat_axis=0, tiled=True
    )
    qkv_keep, qkv_got = together(qkv_keep, qkv_got)

    qkv_keep, qkv_send = halve_add(qkv_keep, qkv_got)
    qkv_keep, qkv_got = halve_on(qkv_keep, qkv_send)
    out_keep, out_got, _ = together(out_keep, out_got, qkv_send)
    out_keep, out_got = halve_on(*halve_add(out_keep, out_got))
    grad_tokens = call(
        norm_pull_kernel, [((rows, width), F32)], tokens, grad_hidden, *sums, gain_in
    )[0]
    result = call(
        result_kernel, [((rows, width), BF)], hidden, result_own, result_got
    )[0]
    qkv_keep, qkv_got, out_keep, out_got, grad_tokens = together(
        qkv_keep, qkv_got, out_keep, out_got, grad_tokens
    )

    got = in_plane_all(finish(w_rows, qkv_keep, qkv_got, gu_keep, gu_got))
    out_rows = to_row_owner(finish_rows(out_keep, out_got), count)
    (grad_w_query, grad_w_key, grad_w_value), grad_norm_gain, head_gain_grads = unpack(
        got, 0, norm_gain, scalars, gains, w_query, w_key, w_value
    )
    (grad_w_gate, grad_w_up), grad_mlp_gain, _ = unpack(
        got, 4 * HEAD_SIZE, mlp_gain, scalars, gains, w_gate, w_up
    )
    return (
        result,
        grad_tokens,
        grad_norm_gain,
        grad_w_query,
        grad_w_key,
        grad_w_value,
        out_rows.astype(F32),
        head_gain_grads[0],
        head_gain_grads[1],
        grad_mlp_gain,
        grad_w_gate,
        grad_w_up,
        down_rows.astype(F32),
    )


def solution(mesh):
    fsdp, seq = mesh.shape["fsdp"], mesh.shape["seq"]
    fine = Mesh(np.asarray(mesh.devices).reshape(fsdp // 4, 2, 2, seq), ALL)
    matrix, vector, group = P(ALL, None), P(ALL), P(ALL[:3], None)
    placed = (
        matrix, vector, matrix, matrix, matrix, matrix, vector, vector, vector,
        matrix, matrix, matrix, group, group, matrix,
    )
    outs = (
        matrix, matrix, vector, matrix, matrix, matrix, matrix, vector, vector, vector,
        matrix, matrix, matrix,
    )
    return jax.shard_map(local, mesh=fine, in_specs=placed, out_specs=outs, check_vma=False)
```

```python
import functools

import jax
import jax.numpy as jnp
import numpy as np
from jax import lax
from jax.experimental import pallas as pl
from jax.experimental.pallas import tpu as pltpu
from jax.sharding import Mesh, PartitionSpec as P

QUERY_HEADS = 16
KEY_VALUE_HEADS = 8
HEAD_SIZE = 128
GROUP = QUERY_HEADS // KEY_VALUE_HEADS
HEADS_WIDTH = GROUP * HEAD_SIZE

EPS = 1e-06
THETA = 1000000.0
SCALE = HEAD_SIZE ** (-0.5)
EXTRA_ROWS = 16

ALL = ("data", "x", "core", "seq")
BF = jnp.bfloat16
F32 = jnp.float32
SWAP = [(0, 1), (1, 0)]


def mm(a, b):
    return lax.dot_general(a, b, (((1,), (0,)), ((), ())), preferred_element_type=F32)


def mm_nt(a, b):
    return lax.dot_general(a, b, (((1,), (1,)), ((), ())), preferred_element_type=F32)


def mm_tn(a, b):
    return lax.dot_general(a, b, (((0,), (0,)), ((), ())), preferred_element_type=F32)


def together(*values):
    return lax.optimization_barrier(values)


def flip(value, axis):
    return lax.ppermute(value, axis, SWAP)


def flip_diagonal(value):
    return lax.ppermute(value, ("x", "seq"), [(i, i ^ 3) for i in range(4)])


def gather_chips(block):
    from_d = flip_diagonal(block)
    return jnp.stack([block, flip(block, "seq"), flip(block, "x"), from_d])


def exchange(own, to_y, to_x, to_d):
    from_d = flip_diagonal(to_d)
    return own, flip(to_y, "seq"), flip(to_x, "x"), from_d


def in_plane_all(payload):
    return lax.all_to_all(payload, ALL[1:], split_axis=0, concat_axis=0, tiled=True)


def to_row_place(block, count):
    route = [(count * j + d, d * 8 + j) for d in range(count) for j in range(8)]
    return lax.ppermute(block, ALL, route)


def doubling_orders(count):
    orders, bit = [[0]], count // 2
    while bit:
        orders.append([o ^ bit for order in orders for o in order])
        bit //= 2
    return orders


def across(value, bit):
    return lax.ppermute(value, "data", [(d, d ^ bit) for d in range(lax.axis_size("data"))])


def double(arrays, last=False):
    arrays, bit = list(arrays), lax.axis_size("data") // 2
    while bit > 1 and not last:
        arrays.append(across(jnp.concatenate(arrays), bit))
        bit //= 2
    if last:
        arrays.append(across(jnp.concatenate(arrays), 1))
    return arrays


def plane_sum(value, *axes):
    for axis in axes or ("core", "x", "seq"):
        value = value + flip(value, axis)
    return value


def data_sum(value, last=False):
    bit = lax.axis_size("data") // 2
    while bit > 1 and not last:
        value = value + across(value, bit)
        bit //= 2
    return value + across(value, 1) if last else value


def to_row_owner(block, count):
    route = [(d * 8 + j, count * j + d) for d in range(count) for j in range(8)]
    return lax.ppermute(block, ALL, route)


def spec(kind, shape, at):
    zeros = (0,) * (len(shape) - 1)
    if kind == "blocks":
        return pl.BlockSpec((2,) + shape[1:], lambda g: (g,) + zeros)
    if kind == "half":
        return pl.BlockSpec((shape[0] // 2,) + shape[1:], lambda g: (g,) + zeros)
    if kind == "group":
        return pl.BlockSpec((shape[0] // 4,) + shape[1:], lambda g: (at + g,) + zeros)
    if kind == "scalars":
        return pl.BlockSpec(memory_space=pltpu.SMEM)
    if kind == "kept":
        return pl.BlockSpec(memory_space=pl.ANY)
    return pl.BlockSpec(shape, lambda g: (0,) + zeros)


def call_half(kernel, which, outs, args, kept=(), scratch=()):
    at = 2 * which
    given = list(args) + [("kept", array) for array in kept]
    aliases = {len(args) + k: k for k in range(len(kept))}
    n_args = len(args)

    def body(*refs):
        kernel(*refs[:n_args], *refs[n_args + len(kept) :])

    return pl.pallas_call(
        body,
        grid=(2,),
        out_shape=tuple(jax.ShapeDtypeStruct(shape, dtype) for _, shape, dtype in outs),
        in_specs=[spec(kind, arg.shape, at) for kind, arg in given],
        out_specs=tuple(spec(kind, shape, at) for kind, shape, _ in outs),
        scratch_shapes=list(scratch),
        input_output_aliases=aliases,
        compiler_params=pltpu.CompilerParams(
            vmem_limit_bytes=24 * 2**20, dimension_semantics=("arbitrary",)
        ),
    )(*[arg for _, arg in given])


def call(kernel, outs, *args):
    vmem = pl.BlockSpec(memory_space=pltpu.VMEM)
    return pl.pallas_call(
        kernel,
        out_shape=tuple(jax.ShapeDtypeStruct(shape, dtype) for shape, dtype in outs),
        in_specs=[vmem for _ in args],
        out_specs=tuple(vmem for _ in outs),
        compiler_params=pltpu.CompilerParams(vmem_limit_bytes=12 * 2**20),
    )(*args)


def whole(*arrays):
    return [("whole", array) for array in arrays]


def pack_kernel(widths, *refs):
    *weights, out = refs
    for j in range(8):
        at = 0
        for width, ref in zip(widths, weights):
            out[j, :, at : at + width] = ref[:, j * width : (j + 1) * width]
            at += width


def pack(*weights):
    widths = [w.shape[1] // 8 for w in weights]
    shape = (8, weights[0].shape[0], sum(widths))
    return pl.pallas_call(
        functools.partial(pack_kernel, widths),
        grid=(1,),
        out_shape=jax.ShapeDtypeStruct(shape, BF),
        in_specs=[spec("whole", w.shape, 0) for w in weights],
        out_specs=spec("whole", shape, 0),
    )(*weights)


def marks_kernel(scalars, norm_gain, mlp_gain, query_gain, key_gain, lengths, seq_order, out):
    width = out.shape[1]

    def placed(ref, at):
        line = ref[...].astype(F32)
        line = jnp.concatenate([line, jnp.zeros((1, width - line.shape[1]), F32)], axis=1)
        return pltpu.roll(line, at * ref.shape[1], 1)

    lines = [placed(ref, scalars[2]) for ref in (norm_gain, mlp_gain, query_gain, key_gain)]
    once = (1 - scalars[1]).astype(F32)
    lines += [placed(ref, scalars[2] // 2) * once for ref in (lengths, seq_order)]
    lines.append(jnp.zeros((2, width), F32))
    out[...] = jnp.concatenate(lines, axis=0).astype(BF)


def make_marks(scalars, width, *values):
    vmem = pl.BlockSpec(memory_space=pltpu.VMEM)
    return pl.pallas_call(
        marks_kernel,
        out_shape=jax.ShapeDtypeStruct((8, width), BF),
        in_specs=[pl.BlockSpec(memory_space=pltpu.SMEM)] + [vmem for _ in values],
        out_specs=vmem,
    )(scalars, *values)


def setup_kernel(n_seq, scalars, marks, gain_in, gain_mid, head_gains, starts):
    rows = marks[...].astype(F32)
    gain_in[...] = rows[0:1]
    gain_mid[...] = rows[1:2]
    head_gains[...] = rows[2:4, :HEAD_SIZE]
    width = rows.shape[1]
    lane = lax.broadcasted_iota(jnp.int32, (1, 128), 1).astype(F32)
    for k, relative in enumerate((0, 2, 1, 3)):
        back = width - lax.bitwise_xor(scalars[2] // 2, relative) * n_seq
        lengths, order = [pltpu.roll(rows[q : q + 1], back, 1)[:, :128] for q in (4, 5)]
        at = jnp.zeros((1, 1), F32)
        for q in range(n_seq):
            starts[k, q : q + 1, :] = jnp.broadcast_to(at, (1, 128))
            mine = (lane == order[:, q : q + 1]) & (lane < n_seq)
            at = at + jnp.sum(jnp.where(mine, lengths, 0.0), axis=1, keepdims=True)
        starts[k, n_seq:, :] = jnp.full((8 - n_seq, 128), 1e9, F32)


def setup(scalars, marks, n_seq):
    width = marks.shape[1]
    outs = [((1, width), F32), ((1, width), F32), ((2, HEAD_SIZE), F32), ((4, 8, 128), F32)]
    vmem = pl.BlockSpec(memory_space=pltpu.VMEM)
    return pl.pallas_call(
        functools.partial(setup_kernel, n_seq),
        out_shape=tuple(jax.ShapeDtypeStruct(shape, dtype) for shape, dtype in outs),
        in_specs=[pl.BlockSpec(memory_space=pltpu.SMEM), vmem],
        out_specs=tuple(vmem for _ in outs),
    )(scalars, marks)


def assemble_kernel(orders, cuts, scalars, *refs):
    arrays, outs = refs[: len(orders)], refs[len(orders) :]
    for order, ref in zip(orders, arrays):
        for k, relative in enumerate(order):
            place, start = lax.bitwise_xor(scalars[0], relative), 0
            for size, out in zip(cuts, outs):
                at = pl.multiple_of(place * size, size)
                out[pl.ds(at, size), :] = ref[k, start : start + size, :]
                start += size


def assemble(arrays, scalars, *cuts):
    count = sum(array.shape[0] for array in arrays)
    orders = doubling_orders(count)
    _, size, width = arrays[0].shape
    cuts = cuts or (size,)
    if any(cut % 16 for cut in cuts):
        came = jnp.concatenate(arrays)
        at = jnp.asarray(np.argsort([o for order in orders for o in order]))
        came = came[at[jnp.arange(count) ^ scalars[0]]]
        ends = np.cumsum(cuts)
        return [came[:, b - a : b].reshape(count * a, width) for a, b in zip(cuts, ends)]
    vmem = pl.BlockSpec(memory_space=pltpu.VMEM)
    return pl.pallas_call(
        functools.partial(assemble_kernel, orders, cuts),
        out_shape=tuple(jax.ShapeDtypeStruct((count * cut, width), BF) for cut in cuts),
        in_specs=[pl.BlockSpec(memory_space=pltpu.SMEM)] + [vmem for _ in arrays],
        out_specs=tuple(vmem for _ in cuts),
    )(scalars, *arrays)


def unpack_kernel(widths, start, scalars, got, gain, *refs):
    weights, outs = refs[: len(widths)], refs[len(widths) : -2]
    gain_out, head_gains = refs[-2:]
    rows, sums, line = gain.shape[0], 0.0, 0.0
    for j in range(8):
        at = start
        for width, weight, out in zip(widths, weights, outs):
            piece = got[j, :rows, at : at + width].astype(F32)
            out[:, j * width : (j + 1) * width] = piece
            kept = weight[:, j * width : (j + 1) * width].astype(F32)
            sums = sums + jnp.sum(piece * kept, axis=1, keepdims=True)
            at += width
        line = line + got[j, rows : rows + 8, : 2 * HEAD_SIZE].astype(F32)
    sums = jnp.broadcast_to(sums / gain[...], (rows, 128))
    gain_out[...] = jnp.transpose(sums)[0:1]
    each = head_gains.shape[1]
    for k in range(2):
        part = line[0:1, k * HEAD_SIZE : (k + 1) * HEAD_SIZE]
        back = lax.rem(HEAD_SIZE - scalars[2] * each, HEAD_SIZE)
        head_gains[k : k + 1, :] = pltpu.roll(part, back, 1)[:, :each]


def unpack(got, start, gain, scalars, gains, *weights):
    widths = [w.shape[1] // 8 for w in weights]
    outs = [(w.shape, F32) for w in weights] + [((1, gain.shape[0]), F32), ((2, gains), F32)]
    vmem = pl.BlockSpec(memory_space=pltpu.VMEM)
    *grads, gain_grad, head_gains = pl.pallas_call(
        functools.partial(unpack_kernel, widths, start),
        out_shape=tuple(jax.ShapeDtypeStruct(shape, dtype) for shape, dtype in outs),
        in_specs=[pl.BlockSpec(memory_space=pltpu.SMEM)] + [vmem] * (2 + len(weights)),
        out_specs=tuple(vmem for _ in outs),
        compiler_params=pltpu.CompilerParams(vmem_limit_bytes=12 * 2**20),
    )(scalars, got, gain.astype(F32)[:, None], *weights)
    return grads, gain_grad[0], head_gains


def merge_kernel(near, other, own, to_y, to_x, to_d):
    own[...] = near[0] + other[0].astype(F32)
    for k, out in ((1, to_y), (2, to_x), (3, to_d)):
        out[...] = (near[k] + other[k].astype(F32)).astype(BF)


def merge_all_kernel(scalars, near, other, own, out):
    own[...] = near[0] + other[0].astype(F32)
    for k in range(4):
        part = near[k] + other[k].astype(F32) if k else jnp.zeros_like(near[0])
        out[lax.bitwise_xor(scalars[3], k)] = part.astype(BF)


def merge_all(scalars, near, other):
    vmem = pl.BlockSpec(memory_space=pltpu.VMEM)
    return pl.pallas_call(
        merge_all_kernel,
        out_shape=(
            jax.ShapeDtypeStruct(near.shape[1:], F32),
            jax.ShapeDtypeStruct(near.shape, BF),
        ),
        in_specs=[pl.BlockSpec(memory_space=pltpu.SMEM), vmem, vmem],
        out_specs=(vmem, vmem),
        compiler_params=pltpu.CompilerParams(vmem_limit_bytes=12 * 2**20),
    )(scalars, near, other)


def merge(near, other):
    shape = near.shape[1:]
    return call(merge_kernel, [(shape, F32)] + [(shape, BF)] * 3, near, other)


def inv_rms(values):
    return lax.rsqrt(jnp.mean(values * values, axis=-1, keepdims=True) + EPS)


def summed(own, from_y, from_x, from_d, rows):
    total = own[:rows]
    for ref in (from_y, from_x, from_d):
        total = total + ref[:rows].astype(F32)
    return total


def hidden_kernel(tokens, own, from_y, from_x, from_d, gain, hidden, normed):
    total = tokens[...].astype(F32) + summed(own, from_y, from_x, from_d, tokens.shape[0])
    hidden[...] = total
    normed[...] = (total * inv_rms(total) * gain[...]).astype(BF)


def result_kernel(hidden, own, others, result):
    total = hidden[...] + own[...]
    for k in range(4):
        total = total + others[k].astype(F32)
    result[...] = total.astype(BF)


def norm_pull_kernel(values, base, own, from_y, from_x, from_d, gain, out, *low):
    v = values[...].astype(F32)
    u = summed(own, from_y, from_x, from_d, v.shape[0]) * gain[...]
    r = inv_rms(v)
    total = base[...].astype(F32) + r * u - v * (r * r * r) * jnp.mean(u * v, -1, keepdims=True)
    out[...] = total
    for ref in low:
        ref[...] = total.astype(BF)


def turn(values, cosine, sine):
    return values * cosine + pltpu.roll(values, HEAD_SIZE // 2, 1) * sine


def turned_mask(starts, in_seq, rows):
    span = 2 * rows

    def ids(dim):
        shape = (span, 1) if dim == 0 else (1, span)
        at = lax.broadcasted_iota(jnp.int32, shape, dim)
        return lax.rem(at + in_seq * rows, span).astype(F32)

    def of_sequence(row_ids):
        return sum((row_ids >= starts[0, k : k + 1, 0:1]).astype(F32) for k in range(8))

    down, along = ids(0), ids(1)
    allowed = (along <= down) & (of_sequence(along) == of_sequence(down))
    return jnp.where(allowed, 0.0, -1e30).astype(F32)


def softmax(query, key, bias):
    scores = mm_nt(query, key) * SCALE + bias
    exp_scores = jnp.exp(scores - jnp.max(scores, axis=-1, keepdims=True))
    return exp_scores / jnp.sum(exp_scores, axis=-1, keepdims=True)


def group_of(blocks, start, rows):
    return jnp.concatenate([blocks[0, start : start + rows, :], blocks[1, start : start + rows, :]])


def split_out(product, rows, parts):
    for k in range(2):
        parts[k, :rows, :] = product[k * rows : (k + 1) * rows].astype(parts.dtype)


def attend_kernel(
    rows, scalars, starts, blocks, weight, gain, head_gains, cosine, sine, *outs
):
    normed, raw, low, attn = outs
    x = group_of(blocks, 0, rows).astype(F32)
    x = (x * inv_rms(x) * gain[...]).astype(BF)
    normed[...] = x
    qkv = mm(x, weight[...])
    raw[...] = qkv[:, : HEADS_WIDTH + HEAD_SIZE]
    cos, sin = cosine[...], sine[...]
    bias = turned_mask(starts, scalars[1], rows)
    heads = []
    for h in range(GROUP + 1):
        part = qkv[:, h * HEAD_SIZE : (h + 1) * HEAD_SIZE]
        norm = head_gains[0:1, :] if h < GROUP else head_gains[1:2, :]
        heads.append(turn(part * inv_rms(part) * norm, cos, sin).astype(BF))
        low[:, h * HEAD_SIZE : (h + 1) * HEAD_SIZE] = heads[-1]
    value = qkv[:, HEADS_WIDTH + HEAD_SIZE :].astype(BF)
    low[:, HEADS_WIDTH + HEAD_SIZE :] = value
    for h in range(GROUP):
        probs = softmax(heads[h], heads[GROUP], bias).astype(BF)
        attn[:, h * HEAD_SIZE : (h + 1) * HEAD_SIZE] = mm(probs, value).astype(BF)


def project_kernel(rows, values, weight, parts):
    split_out(mm(values[...], weight[...]), rows, parts)


def project(values, weight, rows):
    return [
        call_half(
            functools.partial(project_kernel, rows),
            which,
            [("blocks", (4, rows, weight.shape[1]), dtype)],
            [("group", values), ("whole", weight)],
        )[0]
        for which, dtype in ((0, F32), (1, BF))
    ]


def feed_kernel(rows, mid, cot, w_gate, w_up, down, normed, mixed, grad_gu, parts):
    ff = down.shape[0]
    x = group_of(mid, 0, rows)
    normed[...] = x
    gate_pre = mm(x, w_gate[...])
    upward = mm(x, w_up[...])
    grad_mixed = mm_nt(group_of(cot, 0, rows), down[...])
    sigma = 1.0 / (1.0 + jnp.exp(-gate_pre))
    silu = gate_pre * sigma
    mixed[...] = (silu * upward).astype(BF)
    grad_gate = (grad_mixed * upward * sigma * (1.0 + gate_pre * (1.0 - sigma))).astype(BF)
    grad_up = (grad_mixed * silu).astype(BF)
    grad_gu[:, :ff] = grad_gate
    grad_gu[:, ff:] = grad_up
    split_out(mm_nt(grad_gate, w_gate[...]) + mm_nt(grad_up, w_up[...]), rows, parts)


def attend_pull_kernel(
    rows, scalars, starts, blocks, low, raw, head_gains, cosine, sine, weight, grad_qkv, gain_out
):
    grad_attn = mm_nt(group_of(blocks, 0, rows), weight[...]).astype(BF)
    cos, sin = cosine[...], sine[...]
    bias = turned_mask(starts, scalars[1], rows)
    key = low[:, HEADS_WIDTH : HEADS_WIDTH + HEAD_SIZE]
    value = low[:, HEADS_WIDTH + HEAD_SIZE :]
    grads, grad_key, grad_value = [], 0.0, 0.0
    for h in range(GROUP):
        query = low[:, h * HEAD_SIZE : (h + 1) * HEAD_SIZE]
        probs = softmax(query, key, bias)
        grad = grad_attn[:, h * HEAD_SIZE : (h + 1) * HEAD_SIZE]
        grad_probs = mm_nt(grad, value)
        row_dot = jnp.sum(probs * grad_probs, axis=-1, keepdims=True)
        grad_scores = (probs * (grad_probs - row_dot)).astype(BF)
        grads.append(mm(grad_scores, key) * SCALE)
        grad_key = grad_key + mm_tn(grad_scores, query)
        grad_value = grad_value + mm_tn(probs.astype(BF), grad)
    grads.append(grad_key * SCALE)
    gain_sums = [0.0, 0.0]
    for h in range(GROUP + 1):
        spot = slice(h * HEAD_SIZE, (h + 1) * HEAD_SIZE)
        which = 0 if h < GROUP else 1
        back = turn(grads[h], cos, -sin)
        part = raw[:, spot]
        r = inv_rms(part)
        u = back * head_gains[which : which + 1, :]
        gain_sums[which] = gain_sums[which] + jnp.sum(back * part * r, axis=0, keepdims=True)
        pulled = r * u - part * (r * r * r) * jnp.mean(u * part, -1, keepdims=True)
        grad_qkv[:, spot] = pulled.astype(BF)
    grad_qkv[:, HEADS_WIDTH + HEAD_SIZE :] = grad_value.astype(BF)
    sums = jnp.concatenate(gain_sums, axis=1)

    @pl.when(pl.program_id(0) == 0)
    def _():
        gain_out[...] = sums

    @pl.when(pl.program_id(0) > 0)
    def _():
        gain_out[...] += sums


def project_nt_kernel(rows, grad_qkv, weight, parts):
    split_out(mm_nt(grad_qkv[...], weight[...]), rows, parts)


def weigh_kernel(orders, scalars, values, *refs):
    *grads, extra, keep, send, total = refs
    if len(grads) == 1:
        grad = grads[0][...]
    else:
        near, far = [ref[...].reshape(-1, ref.shape[2]) for ref in grads]
        grad = jnp.where(pl.program_id(0) < 2, near, far)
    term = mm_tn(values[...], grad)

    @pl.when(pl.program_id(0) == 0)
    def _():
        total[...] = term

    @pl.when(pl.program_id(0) > 0)
    def _():
        total[...] += term

    size = total.shape[0] // (2 * keep.shape[0])
    more = keep.shape[1] - size

    @pl.when(pl.program_id(0) == pl.num_programs(0) - 1)
    def _():
        for order, out in zip(orders, (keep, send)):
            for k, relative in enumerate(order):
                at = lax.bitwise_xor(scalars[0], relative) * size
                block = total[pl.ds(pl.multiple_of(at, size), size), :]
                if not more:
                    out[k] = block.astype(out.dtype)
                    continue
                line = extra[...]
                rest = total.shape[1] - line.shape[1]
                line = jnp.concatenate([line, jnp.zeros((1, rest), F32)], axis=1)
                line = jnp.broadcast_to(line, (more, total.shape[1]))
                out[k] = jnp.concatenate([block, line], axis=0).astype(out.dtype)


def weigh(values, grads, scalars, count, extra=None):
    more = 0 if extra is None else EXTRA_ROWS
    extra = jnp.zeros((1, 128), F32) if extra is None else extra
    bits = [1 << k for k in range(1, count.bit_length() - 1)]
    evens = [o for o in range(count) if not o & 1]
    evens = sorted(evens, key=lambda o: [bool(o & bit) for bit in bits])
    orders = (evens, [o ^ 1 for o in evens])
    height, width = values.shape[1], grads[0].shape[-1]
    half = (count // 2, height // count + more, width)
    if len(grads) == 1:
        grad_specs = [spec("group", grads[0].shape, 0)]
    else:
        block = (2,) + grads[0].shape[1:]
        grad_specs = [
            pl.BlockSpec(block, lambda g: (jnp.minimum(g, 1), 0, 0)),
            pl.BlockSpec(block, lambda g: (jnp.maximum(g - 2, 0), 0, 0)),
        ]
    return pl.pallas_call(
        functools.partial(weigh_kernel, orders),
        grid=(4,),
        out_shape=(jax.ShapeDtypeStruct(half, F32), jax.ShapeDtypeStruct(half, BF)),
        in_specs=[spec("scalars", (), 0), spec("group", values.shape, 0)]
        + grad_specs
        + [spec("whole", extra.shape, 0)],
        out_specs=(spec("whole", half, 0), spec("whole", half, 0)),
        scratch_shapes=[pltpu.VMEM((height, width), F32)],
        compiler_params=pltpu.CompilerParams(
            vmem_limit_bytes=24 * 2**20, dimension_semantics=("arbitrary",)
        ),
    )(scalars, values, *grads, extra)


def add_kernel(keep, got, kept, send):
    total = keep[...] + got[...].astype(F32)
    size = kept.shape[0]
    kept[...] = total[:size]
    send[...] = total[size:].astype(BF)


def halve_add(keep, got):
    part = (keep.shape[0] // 2,) + keep.shape[1:]
    return call(add_kernel, [(part, F32), (part, BF)], keep, got)


def halve_on(keep, send):
    got, bit = across(send, 2), 4
    while keep.shape[0] > 1:
        keep, send = halve_add(keep, got)
        got = across(send, bit)
        bit *= 2
    return keep, got


def finish_kernel(rows, *refs):
    *terms, out = refs
    at = 0
    for keep, got in zip(terms[::2], terms[1::2]):
        size = 8 * rows
        total = (keep[0, :size, :] + got[0, :size, :].astype(F32)).astype(BF)
        width = total.shape[1]
        for j in range(8):
            out[j, :rows, at : at + width] = total[j * rows : (j + 1) * rows]
            if at == 0:
                line = keep[0, size : size + 8, :] + got[0, size : size + 8, :].astype(F32)
                out[j, rows:, :width] = line.astype(BF)
            else:
                out[j, rows:, at : at + width] = jnp.zeros((8, width), BF)
        at += width


def finish(rows, *terms):
    shape = (8, rows + 8, sum(term.shape[2] for term in terms[::2]))
    return call(functools.partial(finish_kernel, rows), [(shape, BF)], *terms)[0]


def finish_rows_kernel(*refs):
    *terms, out = refs
    at = 0
    for keep, got in zip(terms[::2], terms[1::2]):
        total = (keep[0] + got[0].astype(F32)).astype(BF)
        out[at : at + total.shape[0], :] = total
        at += total.shape[0]


def finish_rows(*terms):
    shape = (sum(term.shape[1] for term in terms[::2]), terms[0].shape[2])
    return call(finish_rows_kernel, [(shape, BF)], *terms)[0]


def local(
    tokens,
    norm_gain,
    w_query,
    w_key,
    w_value,
    w_output,
    query_gain,
    key_gain,
    mlp_gain,
    w_gate,
    w_up,
    w_down,
    lengths,
    seq_order,
    cotangent,
):
    rows, width = tokens.shape
    count = lax.axis_size("data")
    place = lax.axis_index("data")
    in_seq = lax.axis_index("seq")
    in_plane = lax.axis_index("x") * 4 + lax.axis_index("core") * 2 + in_seq
    w_rows = w_query.shape[0]
    gains = query_gain.shape[0]
    n_seq = lengths.shape[1]
    plane_rows = 8 * rows
    me = place * 8 + in_plane
    in_chips = lax.axis_index("x") * 2 + in_seq
    scalars = jnp.stack([place, in_seq, me, in_chips]).astype(jnp.int32)

    half = HEAD_SIZE // 2
    angles = np.arange(2 * rows)[:, None] * THETA ** (-np.arange(half) * (2.0 / HEAD_SIZE))
    turns = np.stack(
        [np.tile(np.cos(angles), 2), np.concatenate([-np.sin(angles), np.sin(angles)], axis=1)]
    ).astype(np.float32)
    turns = jnp.asarray(np.stack([turns, np.roll(turns, -rows, axis=1)]))
    turns = lax.dynamic_index_in_dim(turns, in_seq, 0, False)
    cosine, sine = turns[0], turns[1]

    payload = pack(w_query, w_key, w_value)
    marks = make_marks(
        scalars, width,
        norm_gain[None], mlp_gain[None], query_gain[None], key_gain[None], lengths, seq_order,
    )
    got = in_plane_all(payload).reshape(8 * w_rows, -1)
    marks = data_sum(data_sum(marks), last=True)
    near = gather_chips(tokens)
    row_weights = jnp.concatenate([w_output, w_down])
    got, marks, near, row_weights, cot, gate, up = together(
        got, marks, near, row_weights, cotangent, w_gate, w_up
    )

    qkv = double([got[None]])
    row_weights = to_row_place(row_weights, count)
    marks = plane_sum(marks)
    far = flip(near, "core")
    gate = in_plane_all(pack(gate)).reshape(1, 8 * w_rows, -1)
    qkv, marks, near, far, row_weights, gate, up, cot = together(
        qkv, marks, near, far, row_weights, gate, up, cot
    )

    qkv = double(qkv, last=True)
    row_weights = double([row_weights[None]])
    cot_near = gather_chips(cot)
    gain_in, gain_mid, head_gains, starts = setup(scalars, marks, n_seq)
    up = in_plane_all(pack(up)).reshape(1, 8 * w_rows, -1)
    qkv, gain_in, near, far, row_weights, gate, up, cot_near = together(
        qkv, gain_in, near, far, row_weights, gate, up, cot_near
    )

    cot_far = flip(cot_near, "core")
    qkv_full = assemble(qkv, scalars)[0]
    kept = ()
    for which, blocks in enumerate((near, far)):
        kept = call_half(
            functools.partial(attend_kernel, rows),
            which,
            [
                ("group", (plane_rows, width), BF),
                ("group", (plane_rows, HEADS_WIDTH + HEAD_SIZE), F32),
                ("group", (plane_rows, 4 * HEAD_SIZE), BF),
                ("group", (plane_rows, HEADS_WIDTH), BF),
            ],
            [("scalars", scalars), ("group", starts), ("blocks", blocks)]
            + whole(qkv_full, gain_in, head_gains, cosine, sine),
            kept=kept,
        )
    normed_in, raw, low, attn_low = kept
    row_weights = double(row_weights, last=True)
    gate = double([gate])
    attn_low, row_weights, gate, up = together(attn_low, row_weights, gate, up)

    out_full, down_full = assemble(row_weights, scalars, w_output.shape[0], w_down.shape[0])
    ff = down_full.shape[0]
    part_near, part_far = project(attn_low, out_full, rows)
    sums = exchange(*merge(part_near, flip(part_far, "core")))
    gate = double(gate, last=True)
    up = double([up])
    sums, gate, up = together(sums, gate, up)

    hidden, normed_mid = call(
        hidden_kernel, [((rows, width), F32), ((rows, width), BF)], tokens, *sums, gain_mid
    )
    mid_near = gather_chips(normed_mid)
    gate_full = assemble(gate, scalars)[0]
    up_full = assemble(double(up, last=True), scalars)[0]
    mid_near, gate_full, up_full = together(mid_near, gate_full, up_full)
    u_parts, kept = [], ()
    mid_far = flip(mid_near, "core")
    for which, mid, cot, dtype in (
        (0, mid_near, cot_near, F32),
        (1, mid_far, cot_far, BF),
    ):
        *kept, u_part = call_half(
            functools.partial(feed_kernel, rows),
            which,
            [
                ("group", (plane_rows, width), BF),
                ("group", (plane_rows, ff), BF),
                ("group", (plane_rows, 2 * ff), BF),
                ("blocks", (4, rows, width), dtype),
            ],
            [("blocks", mid), ("blocks", cot)] + whole(gate_full, up_full, down_full),
            kept=kept,
        )
        u_parts.append(u_part)
    mid_all, mixed, grad_gu = kept
    sums = exchange(*merge(u_parts[0], flip(u_parts[1], "core")))
    down_keep, down_send = weigh(mixed, [cot_near, cot_far], scalars, count)
    down_got = across(down_send, 1)
    mid_all, _ = together(mid_all, down_send)
    gu_keep, gu_send = weigh(mid_all, [grad_gu], scalars, count)
    result_near, result_far = project(mixed, down_full, rows)
    result_own, result_parts = merge_all(scalars, result_near, flip(result_far, "core"))
    sums, result_own, result_parts, gu_send, down_got = together(
        sums, result_own, result_parts, gu_send, down_got
    )

    grad_hidden, grad_out = call(
        norm_pull_kernel,
        [((rows, width), F32), ((rows, width), BF)],
        hidden, cotangent, *sums, gain_mid,
    )
    out_near = gather_chips(grad_out)
    gu_got = across(gu_send, 1)
    down_keep, down_got = halve_on(*halve_add(down_keep, down_got))
    gu_keep, gu_send = halve_add(gu_keep, gu_got)
    out_near, gu_keep, gu_send, down_keep, down_got = together(
        out_near, gu_keep, gu_send, down_keep, down_got
    )

    out_far = flip(out_near, "core")
    gu_keep, gu_got = halve_on(gu_keep, gu_send)
    down_rows = to_row_owner(finish_rows(down_keep, down_got), count)
    gain_parts, kept = [], ()
    for which, blocks in enumerate((out_near, out_far)):
        *kept, gain_part = call_half(
            functools.partial(attend_pull_kernel, rows),
            which,
            [
                ("group", (plane_rows, 4 * HEAD_SIZE), BF),
                ("whole", (1, 2 * HEAD_SIZE), F32),
            ],
            [("scalars", scalars), ("group", starts), ("blocks", blocks)]
            + [("group", low), ("group", raw)]
            + whole(head_gains, cosine, sine, out_full),
            kept=kept,
        )
        gain_parts.append(gain_part)
    grad_qkv = kept[0]
    gains_sum = gain_parts[0] + gain_parts[1]
    qkv_keep, qkv_send = weigh(normed_in, [grad_qkv], scalars, count, gains_sum)
    part_near, part_far = [
        call_half(
            functools.partial(project_nt_kernel, rows),
            which,
            [("blocks", (4, rows, width), dtype)],
            [("group", grad_qkv)] + whole(qkv_full),
        )[0]
        for which, dtype in ((0, F32), (1, BF))
    ]
    part_near, part_far, qkv_keep, qkv_send, attn_low, down_rows, gu_keep, gu_got = together(
        part_near, part_far, qkv_keep, qkv_send, attn_low, down_rows, gu_keep, gu_got
    )

    qkv_got = across(qkv_send, 1)
    sums = exchange(*merge(part_near, flip(part_far, "core")))
    out_keep, out_send = weigh(attn_low, [out_near, out_far], scalars, count)
    out_got = across(out_send, 1)
    result_got = lax.all_to_all(
        result_parts, ("x", "seq"), split_axis=0, concat_axis=0, tiled=True
    )
    qkv_keep, qkv_got = together(qkv_keep, qkv_got)

    qkv_keep, qkv_send = halve_add(qkv_keep, qkv_got)
    qkv_keep, qkv_got = halve_on(qkv_keep, qkv_send)
    out_keep, out_got, _ = together(out_keep, out_got, qkv_send)
    out_keep, out_got = halve_on(*halve_add(out_keep, out_got))
    grad_tokens = call(
        norm_pull_kernel, [((rows, width), F32)], tokens, grad_hidden, *sums, gain_in
    )[0]
    result = call(
        result_kernel, [((rows, width), BF)], hidden, result_own, result_got
    )[0]
    qkv_keep, qkv_got, out_keep, out_got, grad_tokens = together(
        qkv_keep, qkv_got, out_keep, out_got, grad_tokens
    )

    got = in_plane_all(finish(w_rows, qkv_keep, qkv_got, gu_keep, gu_got))
    out_rows = to_row_owner(finish_rows(out_keep, out_got), count)
    (grad_w_query, grad_w_key, grad_w_value), grad_norm_gain, head_gain_grads = unpack(
        got, 0, norm_gain, scalars, gains, w_query, w_key, w_value
    )
    (grad_w_gate, grad_w_up), grad_mlp_gain, _ = unpack(
        got, 4 * HEAD_SIZE, mlp_gain, scalars, gains, w_gate, w_up
    )
    return (
        result,
        grad_tokens,
        grad_norm_gain,
        grad_w_query,
        grad_w_key,
        grad_w_value,
        out_rows.astype(F32),
        head_gain_grads[0],
        head_gain_grads[1],
        grad_mlp_gain,
        grad_w_gate,
        grad_w_up,
        down_rows.astype(F32),
    )


def solution(mesh):
    fsdp, seq = mesh.shape["fsdp"], mesh.shape["seq"]
    fine = Mesh(np.asarray(mesh.devices).reshape(fsdp // 4, 2, 2, seq), ALL)
    matrix, vector, group = P(ALL, None), P(ALL), P(ALL[:3], None)
    placed = (
        matrix, vector, matrix, matrix, matrix, matrix, vector, vector, vector,
        matrix, matrix, matrix, group, group, matrix,
    )
    outs = (
        matrix, matrix, vector, matrix, matrix, matrix, matrix, vector, vector, vector,
        matrix, matrix, matrix,
    )
    return jax.shard_map(local, mesh=fine, in_specs=placed, out_specs=outs, check_vma=False)
```
